512 devices in a mesh: replica: 32 (over z, y_hi, core), fsdp: 16 (over x, y_lo).
Axes of the slice: x: 4, y: 8 (y_hi: 2, y_lo: 4; y = y_hi * 4 + y_lo), z: 8, core: 2. Of those that a mesh axis runs over, the one named last changes fastest.
Arguments:
- patch_rows: bfloat16 [512, 256, 1792], P(('replica', 'fsdp'))
- qkv_weight: bfloat16 [32, 1792, 2688], P('replica', 'fsdp')
- out_weight: bfloat16 [32, 896, 1792], P('replica', 'fsdp'), may hold values from -0.1875 to 0.1875
- cotangent: bfloat16 [512, 256, 1792], P(('replica', 'fsdp')), may hold values from -6 to 6
- keep_mask: int32 [512, 256], P(('replica', 'fsdp')), may hold values from 0 to 1, as said below
- outer_delta: float32 [32, 2, 524288], P('replica', None, 'fsdp'), may hold values from -6 to 6
- momentum: float32 [2, 524288], P(None, 'fsdp'), may hold values from -6 to 6
- global_params: float32 [2, 524288], P(None, 'fsdp'), may hold values from -6 to 6
- fragment_index: int32 [1], replicated, may hold values from 0 to 1
Outputs:
- layer_out: bfloat16 [512, 256, 1792], P(('replica', 'fsdp'))
- out_grad: float32 [32, 896, 1792], P('replica', 'fsdp')
- new_momentum: float32 [524288], P('fsdp')
- new_params: float32 [524288], P('fsdp')
The draws below stay inside these ranges and needn't reach their ends.
Inputs may be any that keep to these rules, and one draw needn't show every extreme that they name: `keep_mask`: each image has exactly 154 kept patches.
All inputs are finite; a program needn't handle non-finite values.
Results may differ from the reference program's by a relative error of at most 0.022.
Values may be sent and summed in bfloat16 or wider, within the bound.
A program may use at most 128 MiB of HBM per device.

```python
import math
import jax
import jax.numpy as jnp
from jax import lax

D = 1792
HSZ = 112
HEADS = 8
HD = 896
P_SIZE = 256
KEEP = 154
IMG_DEV = 1
IMAGES = 512
NFRAG = 2
FRAG = 524288
N_REPLICA = 32
N_FSDP = 16


def draw_patch_rows(key, part):
    key = jax.random.fold_in(key, 1)
    base = jax.random.normal(key, (IMAGES, P_SIZE, D), jnp.float32)
    return base.astype(jnp.bfloat16)


def draw_qkv_weight(key, part):
    key = jax.random.fold_in(key, 2)
    weight = jax.random.normal(key, (N_REPLICA, D, 3 * HD), jnp.float32) * D ** (-0.5)
    return weight.astype(jnp.bfloat16)


def draw_keep_mask(key, part):
    key = jax.random.fold_in(key, 3)
    keys = jax.random.split(key, IMAGES)
    orders = jax.vmap(lambda single: jax.random.permutation(single, P_SIZE))(keys)
    return (orders < KEEP).astype(jnp.int32)


def shard_levels(own_key, shape, cuts, low, top_value):
    factor_of = 1.0
    for dim, shards_of in cuts:
        heights = jax.random.uniform(jax.random.fold_in(jax.random.fold_in(own_key, 6), dim), (shards_of,), jnp.float32, low / len(cuts), top_value / len(cuts))
        factor_of = factor_of * jnp.repeat(jnp.exp(heights), shape[dim] // shards_of).reshape((-1,) + (1,) * (len(shape) - 1 - dim))
    return factor_of


def scatter_about(rng, shape, scale, bound, pieces=(), held_as=jnp.bfloat16):
    factor_of = shard_levels(rng, shape, pieces, -0.22, 0.18) if pieces else 1.0
    array = jax.random.normal(rng, shape, jnp.float32) * scale * factor_of
    return jnp.minimum(jnp.maximum(array, -bound), bound).astype(held_as)


def setup_inputs(seed: int = 0) -> dict:
    splits = jax.random.split(jax.random.key(seed), 10)
    patch_rows = draw_patch_rows(jax.random.fold_in(splits[9], 71), 0)
    qkv_weight = draw_qkv_weight(jax.random.fold_in(splits[9], 71), 0)
    out_weight = scatter_about(splits[2], (N_REPLICA, HD, D), HD ** -0.5, 0.1875, ((0, 32), (1, 16)))
    cotangent = scatter_about(splits[3], (IMAGES, P_SIZE, D), 1.0, 6.0, ((0, 512),))
    keep_mask = draw_keep_mask(jax.random.fold_in(splits[9], 71), 0)
    outer_delta = scatter_about(splits[5], (N_REPLICA, NFRAG, FRAG), 1.0, 6.0, ((0, 32), (2, 16)), jnp.float32)
    momentum = scatter_about(splits[6], (NFRAG, FRAG), 1.0, 6.0, ((1, 16),), jnp.float32)
    global_params = scatter_about(splits[7], (NFRAG, FRAG), 1.0, 6.0, ((1, 16),), jnp.float32)
    fragment_index = jax.random.randint(splits[8], (1,), 0, NFRAG).astype(jnp.int32)
    return {"patch_rows": patch_rows, "qkv_weight": qkv_weight, "out_weight": out_weight, "cotangent": cotangent, "keep_mask": keep_mask, "outer_delta": outer_delta, "momentum": momentum, "global_params": global_params, "fragment_index": fragment_index}


EPS = 1e-06

def layer_norm(values):
    floats = values.astype(jnp.float32)
    centre = lax.optimization_barrier(jnp.mean(floats, axis=-1, keepdims=True))
    shifted = floats - centre
    spread = lax.optimization_barrier(jnp.mean(shifted * shifted, axis=-1, keepdims=True))
    return (shifted * lax.rsqrt(spread + EPS)).astype(jnp.bfloat16)

def attend(qkv_rows, keep):
    query = qkv_rows[:, :, 0].astype(jnp.float32)
    keys = qkv_rows[:, :, 1].astype(jnp.float32)
    value_rows = qkv_rows[:, :, 2].astype(jnp.float32)
    scores = jnp.einsum('iqhd,ikhd->ihqk', query, keys) * (1.0 / math.sqrt(HSZ))
    scores = jnp.where(keep[:, None, None, :] > 0, scores, -1e+30)
    peak = lax.optimization_barrier(jnp.max(scores, axis=-1, keepdims=True))
    expo = jnp.exp(scores - peak)
    total = lax.optimization_barrier(jnp.sum(expo, axis=-1, keepdims=True))
    probs = (expo / total).astype(jnp.bfloat16)
    mixed = jnp.einsum('ihqk,ikhd->iqhd', probs.astype(jnp.float32), value_rows).astype(jnp.bfloat16)
    mixed = mixed.reshape(mixed.shape[0], mixed.shape[1], HD)
    return mixed * keep[:, :, None].astype(jnp.bfloat16)

def reference(patch_rows, qkv_weight, out_weight, cotangent, keep_mask, outer_delta, momentum, global_params, fragment_index):
    group = N_FSDP * IMG_DEV

    def one_replica(items):
        rows, weight_in, weight_out, grads, keep = items
        normed = layer_norm(rows)
        qkv_rows = jnp.dot(normed.reshape(-1, D), weight_in, preferred_element_type=jnp.float32).astype(jnp.bfloat16)
        qkv_rows = qkv_rows.reshape(group, P_SIZE, 3, HEADS, HSZ)
        attended = attend(qkv_rows, keep)
        result = jnp.dot(attended.reshape(-1, HD), weight_out, preferred_element_type=jnp.float32).astype(jnp.bfloat16)
        result = result.reshape(group, P_SIZE, D)
        left = attended.reshape(N_FSDP, IMG_DEV * P_SIZE, HD).astype(jnp.float32)
        right = grads.reshape(N_FSDP, IMG_DEV * P_SIZE, D).astype(jnp.float32)
        partial_terms = jnp.einsum('fth,ftd->fhd', left, right)
        rounded = lax.optimization_barrier(partial_terms.astype(jnp.bfloat16))
        return (result, lax.optimization_barrier(jnp.sum(rounded.astype(jnp.float32), axis=0)))
    outputs, out_grad = lax.map(one_replica, (patch_rows.reshape(N_REPLICA, group, P_SIZE, D), qkv_weight, out_weight, cotangent.reshape(N_REPLICA, group, P_SIZE, D), keep_mask.reshape(N_REPLICA, group, P_SIZE)))
    layer_out = outputs.reshape(IMAGES, P_SIZE, D)
    index = fragment_index[0].astype(jnp.int32)
    chosen = lax.dynamic_index_in_dim(outer_delta, index, 1, keepdims=False)
    average = lax.optimization_barrier(jnp.sum(chosen, axis=0)) / N_REPLICA
    old_momentum = lax.dynamic_index_in_dim(momentum, index, 0, keepdims=False)
    old_params = lax.dynamic_index_in_dim(global_params, index, 0, keepdims=False)
    new_momentum = 0.9 * old_momentum + average
    new_params = old_params - 0.7 * (average + 0.9 * new_momentum)
    return (layer_out, out_grad, new_momentum, new_params)
```

```python
import math

import jax
import jax.numpy as jnp
from jax import lax
from jax.experimental import pallas as pl
from jax.experimental.pallas import tpu as pltpu
from jax.sharding import PartitionSpec as P

HSZ = 112
HEADS = 8
KEEP = 154
ROWS = 160
HALF = ROWS // 2
NX = 4
NY = 4
EPS = 1e-06
MESH = pl.DeviceIdType.MESH
F32 = jnp.float32
BF16 = jnp.bfloat16


def dot(a, b, dims=(((1,), (0,)), ((), ()))):
    return lax.dot_general(a, b, dims, preferred_element_type=F32)


def kernel(
    patch_ref, qkvw_ref, outw_ref, cot_ref, mask_ref, delta_ref, mom_ref, par_ref,
    out_ref, grad_ref, newm_ref, newp_ref,
    pick, wpack, wbuf, act, cotb, owbuf, qkv, att, lo_send, lo_recv, g_send, g_recv,
    sum1, sum2, rec1, rec2, rec3, total,
    wx_s, wx_r, wy_s, wy_r, wf_s, ax_s, ax_r, cx_s, cx_r, oy_s, oy_r, of_s,
    lx_s, lx_r, gy_s, gy_r, pc_s, pc_r, z1_s, z1_r, z2_s, z2_r,
):
    r = lax.axis_index("replica")
    f = lax.axis_index("fsdp")
    nz = lax.axis_size("replica") // 4
    core, y_hi, z = lax.rem(r, 2), lax.rem(r // 2, 2), r // 4
    x, y = f // NY, lax.rem(f, NY)
    r_core = r + 1 - 2 * core
    r_yhi = r + 2 - 4 * y_hi

    def at_x(k):
        return lax.rem(x + k, NX)

    def at_y(k):
        return lax.rem(y + k, NY)

    def dev_x(k):
        return (r, at_x(k) * NY + y)

    def dev_y(yy):
        return (r, x * NY + yy)

    def dev_z(k):
        return (lax.rem(z + k, nz) * 4 + lax.rem(r, 4), f)

    def remote(src, dst, s, t, dev):
        return pltpu.make_async_remote_copy(
            src_ref=src, dst_ref=dst, send_sem=s, recv_sem=t, device_id=dev, device_id_type=MESH
        )

    barrier = pltpu.get_barrier_semaphore()
    partners = [dev_x(k) for k in (1, 2, 3)] + [dev_y(at_y(k)) for k in (1, 2, 3)]
    partners += [(r_core, f), (r_yhi, f)] + [dev_z(k) for k in range(1, nz)]
    for dev in partners:
        pl.semaphore_signal(barrier, inc=1, device_id=dev, device_id_type=MESH)

    for k in range(NX):
        start = min(224 * k // 128, 4) * 128
        row = lax.broadcasted_iota(jnp.int32, (384, 256), 0)
        lane = lax.broadcasted_iota(jnp.int32, (384, 256), 1)
        wanted = 224 * k - start + 56 * (lane // 64) + lane % 64
        chosen = jnp.where((row == wanted) & (lane % 64 < 56), 1.0, 0.0).astype(BF16)
        for t in range(3):
            cols = qkvw_ref[:, 896 * t + start : 896 * t + start + 384]
            wpack[k, :, 256 * t : 256 * t + 256] = dot(cols, chosen).astype(BF16)
    wbuf[f] = wpack[x]
    owbuf[y, 0:56, :] = outw_ref[...]
    owbuf[y, 56:64, :] = jnp.zeros((8, outw_ref.shape[1]), BF16)

    pl.semaphore_wait(barrier, len(partners))

    def w_x(k):
        return remote(wpack.at[at_x(k)], wbuf.at[f], wx_s.at[k], wx_r.at[NX - k], dev_x(k))

    def w_x_in(k):
        slot = wbuf.at[at_x(k) * NY + y]
        return remote(slot, slot, wx_s.at[NX - k], wx_r.at[k], dev_x(k))

    def along_y(buf, send, recv, fwd):
        def out(k):
            to = at_y(k)
            return remote(buf(y), buf(y), send(k), recv(y), dev_y(to))

        def near(k):
            return jnp.abs(at_y(k) - y) < 3

        def start():
            for k in (1, 3, 2):
                pl.when(near(k))(lambda k=k: out(k).start())

        def forward():
            def from_low():
                remote(buf(0), buf(0), fwd, recv(0), dev_y(3)).wait_recv()
                remote(buf(0), buf(0), fwd, recv(0), dev_y(3)).start()

            def from_high():
                remote(buf(3), buf(3), fwd, recv(3), dev_y(0)).wait_recv()
                remote(buf(3), buf(3), fwd, recv(3), dev_y(0)).start()

            pl.when(y == 2)(from_low)
            pl.when(y == 1)(from_high)

        def finish():
            for k in (1, 2, 3):
                src = at_y(k)
                done = ((y == 2) & (src == 0)) | ((y == 1) & (src == 3))
                pl.when(jnp.logical_not(done))(
                    lambda src=src: remote(buf(src), buf(src), fwd, recv(src), dev_y(src)).wait_recv()
                )

        def drain():
            for k in (1, 3, 2):
                pl.when(near(k))(lambda k=k: out(k).wait_send())
            pl.when((y == 1) | (y == 2))(
                lambda: remote(buf(y), buf(y), fwd, recv(y), dev_y(at_y(1))).wait_send()
            )

        return start, forward, finish, drain

    w_y = [
        along_y(
            lambda yy, k=k: wbuf.at[at_x(k) * NY + yy],
            lambda j, k=k: wy_s.at[k, j],
            lambda yy, k=k: wy_r.at[k, yy],
            wf_s.at[k],
        )
        for k in range(NX)
    ]
    o_y = along_y(lambda yy: owbuf.at[yy], lambda j: oy_s.at[j], lambda yy: oy_r.at[yy], of_s)

    for k in (2, 1, 3):
        w_x(k).start()
    w_y[0][0]()

    mask = mask_ref[...]
    n = mask.shape[1]
    upper = (
        lax.broadcasted_iota(jnp.int32, (n, n), 0) <= lax.broadcasted_iota(jnp.int32, (n, n), 1)
    )
    place = dot(
        jnp.broadcast_to(mask, (16, n)).astype(F32).astype(BF16),
        jnp.where(upper, 1.0, 0.0).astype(BF16),
    )[0:1, :].astype(jnp.int32)
    place = jnp.where(mask > 0, place - 1, -1)
    pick[...] = jnp.where(
        lax.broadcasted_iota(jnp.int32, (ROWS, n), 0) == place, 1.0, 0.0
    ).astype(BF16)
    kept = dot(pick[...], patch_ref[...])
    shifted = kept - jnp.mean(kept, axis=-1, keepdims=True)
    spread = jnp.mean(shifted * shifted, axis=-1, keepdims=True)
    act[x] = (shifted * lax.rsqrt(spread + EPS)).astype(BF16)

    low, high = pl.ds(0, HALF), pl.ds(HALF, HALF)

    def along_x(buf, send, recv):
        def move(i, who, rows, to):
            return remote(buf.at[who, rows], buf.at[who, rows], send.at[i], recv.at[i], dev_x(to))

        def own():
            return [move(0, x, low, 1), move(1, x, high, 3), move(2, x, high, 1), move(3, x, low, 3)]

        def passing():
            return [move(4, at_x(3), low, 1), move(5, at_x(1), high, 3)]

        def incoming():
            return [
                move(0, at_x(3), low, 3), move(1, at_x(1), high, 1),
                move(2, at_x(3), high, 3), move(3, at_x(1), low, 1),
                move(4, at_x(2), low, 2), move(5, at_x(2), high, 2),
            ]

        def start():
            for c in own():
                c.start()

        def forward():
            got = incoming()
            for i in (0, 1):
                got[i].wait_recv()
                passing()[i].start()

        def finish():
            for c in incoming()[2:]:
                c.wait_recv()

        def drain():
            for c in own() + passing():
                c.wait_send()

        return start, forward, finish, drain

    a_x = along_x(act, ax_s, ax_r)
    c_x = along_x(cotb, cx_s, cx_r)
    a_x[0]()

    def rows8(at, size):
        return pl.ds(pl.multiple_of(at, 8), size)

    pair1 = remote(delta_ref.at[rows8(128 * (1 - core), 128)], rec1, pc_s.at[0], pc_r.at[0], (r_core, f))
    pair1.start()

    for k in (1, 3, 2):
        w_x_in(k).wait_recv()
        w_y[k][0]()

    cotb[x] = dot(pick[...], cot_ref[...]).astype(BF16)
    pair1.wait_recv()
    sum1[...] = delta_ref[rows8(128 * core, 128), :] + rec1[...]
    pair2 = remote(sum1.at[rows8(64 * (1 - y_hi), 64)], rec2, pc_s.at[1], pc_r.at[1], (r_yhi, f))
    pair2.start()

    a_x[1]()
    w_y[0][1]()
    c_x[0]()
    pair2.wait_recv()
    sum2[...] = sum1[rows8(64 * y_hi, 64), :] + rec2[...]

    def z_out(k):
        to = lax.rem(z + k, nz)
        return remote(sum2.at[rows8(8 * to, 8)], rec3.at[nz - k], z1_s.at[k], z1_r.at[nz - k], dev_z(k))

    for k in range(1, nz):
        z_out(k).start()
    w_y[1][1]()
    w_y[3][1]()

    def z_in(k):
        return remote(rec3.at[k], rec3.at[k], z1_s.at[nz - k], z1_r.at[k], dev_z(k))

    mine = sum2[rows8(8 * z, 8), :]
    for k in range(1, nz):
        z_in(k).wait_recv()
        mine = mine + rec3[k]
    base = 128 * core + 64 * y_hi
    total[rows8(base + 8 * z, 8), :] = mine

    def z_back(k):
        part = total.at[rows8(base + 8 * z, 8)]
        return remote(part, part, z2_s.at[k], z2_r.at[nz - k], dev_z(k))

    def z_back_in(k):
        part = total.at[rows8(base + 8 * lax.rem(z + k, nz), 8)]
        return remote(part, part, z2_s.at[nz - k], z2_r.at[k], dev_z(k))

    for k in range(1, nz):
        z_back(k).start()
    w_y[2][1]()
    o_y[0]()
    c_x[1]()

    for k in range(1, nz):
        z_back_in(k).wait_recv()

    def two_out(i, at, size, dev):
        part = total.at[rows8(at, size)]
        return remote(part, part, pc_s.at[i], pc_r.at[i], dev)

    pair3 = two_out(2, base, 64, (r_yhi, f))
    pair3.start()
    two_out(2, 128 * core + 64 * (1 - y_hi), 64, (r_yhi, f)).wait_recv()
    pair4 = two_out(3, 128 * core, 128, (r_core, f))
    pair4.start()
    two_out(3, 128 * (1 - core), 128, (r_core, f)).wait_recv()
    average = total[...] * (1.0 / 32.0)
    new_m = 0.9 * mom_ref[...] + average
    newm_ref[...] = new_m
    newp_ref[...] = par_ref[...] - 0.7 * (average + 0.9 * new_m)
    o_y[1]()

    a_x[2]()
    for k in range(NX):
        w_y[k][2]()
    width = act.shape[2]
    qkv[...] = dot(
        act[...].reshape(NX * ROWS, width), wbuf[...].reshape(width, 768)
    ).astype(BF16).reshape(NX, ROWS, 768)

    def attend(i, carry):
        for h in range(2):
            q = qkv[i, :, 128 * h : 128 * h + 128]
            key = qkv[i, :, 256 + 128 * h : 384 + 128 * h]
            val = qkv[i, :, 512 + 128 * h : 640 + 128 * h]
            scores = dot(q, key, (((1,), (1,)), ((), ()))) * (1.0 / math.sqrt(HSZ))
            col = lax.broadcasted_iota(jnp.int32, (ROWS, ROWS), 1)
            scores = jnp.where(col < KEEP, scores, -1e30)
            expo = jnp.exp(scores - jnp.max(scores, axis=-1, keepdims=True))
            probs = (expo / jnp.sum(expo, axis=-1, keepdims=True)).astype(BF16)
            att[i, :, 128 * h : 128 * h + 128] = dot(probs, val).astype(BF16)
        return carry

    lax.fori_loop(0, NX, attend, 0)

    o_y[2]()
    def project(i, carry):
        lo_send[i] = dot(att[i], owbuf[...].reshape(NY * 64, width)).astype(BF16)
        return carry

    lax.fori_loop(0, NX, project, 0)

    def lo_out(k):
        return remote(lo_send.at[at_x(k)], lo_recv.at[NX - k], lx_s.at[k], lx_r.at[NX - k], dev_x(k))

    def lo_in(k):
        return remote(lo_recv.at[k], lo_recv.at[k], lx_s.at[NX - k], lx_r.at[k], dev_x(k))

    for k in (2, 1, 3):
        lo_out(k).start()

    c_x[2]()
    g_send[...] = dot(
        att[...].reshape(NX * ROWS, 256), cotb[...].reshape(NX * ROWS, width), (((0,), (0,)), ((), ()))
    ).astype(BF16).reshape(NY, 64, width)

    def g_out(k):
        return remote(g_send.at[at_y(k)], g_recv.at[NY - k], gy_s.at[k], gy_r.at[NY - k], dev_y(at_y(k)))

    def g_in(k):
        return remote(g_recv.at[k], g_recv.at[k], gy_s.at[NY - k], gy_r.at[k], dev_y(at_y(k)))

    for k in (2, 1, 3):
        g_out(k).start()

    whole = g_send[y].astype(F32)
    for k in (1, 2, 3):
        g_in(k).wait_recv()
        whole = whole + g_recv[k].astype(F32)
    grad_ref[...] = whole[0:56, :]

    result = lo_send[x].astype(F32)
    for k in (1, 3, 2):
        lo_in(k).wait_recv()
        result = result + lo_recv[k].astype(F32)
    out_ref[...] = dot(pick[...], result.astype(BF16), (((0,), (0,)), ((), ()))).astype(BF16)

    for k in (1, 2, 3):
        w_x(k).wait_send()
        lo_out(k).wait_send()
        g_out(k).wait_send()
    for k in range(NX):
        w_y[k][3]()
    o_y[3]()
    a_x[3]()
    c_x[3]()
    for c in (pair1, pair2, pair3, pair4):
        c.wait_send()
    for k in range(1, nz):
        z_out(k).wait_send()
        z_back(k).wait_send()


def on_device(
    patch_rows, qkv_weight, out_weight, cotangent, keep_mask, outer_delta, momentum, global_params,
    fragment_index,
):
    index = fragment_index[0]
    delta = lax.dynamic_index_in_dim(outer_delta[0], index, 0, keepdims=False).reshape(256, 128)
    old_m = lax.dynamic_index_in_dim(momentum, index, 0, keepdims=False).reshape(256, 128)
    old_p = lax.dynamic_index_in_dim(global_params, index, 0, keepdims=False).reshape(256, 128)
    width = patch_rows.shape[2]
    nz = lax.axis_size("replica") // 4
    vmem = pl.BlockSpec(memory_space=pltpu.VMEM)
    sem = pltpu.SemaphoreType.DMA
    shapes = [
        jax.ShapeDtypeStruct((256, width), BF16),
        jax.ShapeDtypeStruct((56, width), F32),
        jax.ShapeDtypeStruct((256, 128), F32),
        jax.ShapeDtypeStruct((256, 128), F32),
    ]
    out, grad, new_m, new_p = pl.pallas_call(
        kernel,
        out_shape=shapes,
        in_specs=[vmem] * 8,
        out_specs=[vmem] * 4,
        scratch_shapes=[
            pltpu.VMEM((ROWS, 256), BF16),
            pltpu.VMEM((NX, 112, 768), BF16),
            pltpu.VMEM((NX * NY, 112, 768), BF16),
            pltpu.VMEM((NX, ROWS, width), BF16),
            pltpu.VMEM((NX, ROWS, width), BF16),
            pltpu.VMEM((NY, 64, width), BF16),
            pltpu.VMEM((NX, ROWS, 768), BF16),
            pltpu.VMEM((NX, ROWS, 256), BF16),
            pltpu.VMEM((NX, ROWS, width), BF16),
            pltpu.VMEM((NX, ROWS, width), BF16),
            pltpu.VMEM((NY, 64, width), BF16),
            pltpu.VMEM((NY, 64, width), BF16),
            pltpu.VMEM((128, 128), F32),
            pltpu.VMEM((64, 128), F32),
            pltpu.VMEM((128, 128), F32),
            pltpu.VMEM((64, 128), F32),
            pltpu.VMEM((nz, 8, 128), F32),
            pltpu.VMEM((256, 128), F32),
            sem((NX,)), sem((NX,)),
            sem((NX, NY)), sem((NX, NY)), sem((NX,)),
            sem((6,)), sem((6,)), sem((6,)), sem((6,)),
            sem((NY,)), sem((NY,)), sem,
            sem((NX,)), sem((NX,)), sem((NY,)), sem((NY,)),
            sem((4,)), sem((4,)), sem((nz,)), sem((nz,)), sem((nz,)), sem((nz,)),
        ],
        compiler_params=pltpu.CompilerParams(
            collective_id=0, has_side_effects=True, vmem_limit_bytes=48 * 1024 * 1024
        ),
    )(
        patch_rows[0], qkv_weight[0], out_weight[0], cotangent[0], keep_mask, delta, old_m, old_p
    )
    return out[None], grad[None], new_m.reshape(-1), new_p.reshape(-1)


def solution(mesh):
    in_specs = (
        P(("replica", "fsdp"), None, None),
        P("replica", "fsdp", None),
        P("replica", "fsdp", None),
        P(("replica", "fsdp"), None, None),
        P(("replica", "fsdp"), None),
        P("replica", None, "fsdp"),
        P(None, "fsdp"),
        P(None, "fsdp"),
        P(),
    )
    out_specs = (
        P(("replica", "fsdp"), None, None),
        P("replica", "fsdp", None),
        P("fsdp"),
        P("fsdp"),
    )
    return jax.shard_map(
        on_device, mesh=mesh, in_specs=in_specs, out_specs=out_specs, check_vma=False
    )
```

```python
import math

import jax
import jax.numpy as jnp
from jax import lax
from jax.experimental import pallas as pl
from jax.experimental.pallas import tpu as pltpu
from jax.sharding import PartitionSpec as P

HSZ = 112
HEADS = 8
KEEP = 154
ROWS = 160
HALF = ROWS // 2
NX = 4
NY = 4
EPS = 1e-06
MESH = pl.DeviceIdType.MESH
F32 = jnp.float32
BF16 = jnp.bfloat16


def dot(a, b, dims=(((1,), (0,)), ((), ()))):
    return lax.dot_general(a, b, dims, preferred_element_type=F32)


def kernel(
    patch_hbm, qkvw_hbm, outw_hbm, cot_hbm, delta_hbm, mom_hbm, par_hbm, mask_ref, index_ref,
    out_ref, grad_ref, newm_ref, newp_ref,
    patch_ref, qkvw_ref, outw_ref, cot_ref, delta_ref, mom_ref, par_ref,
    local, piece, from_y, parts, total,
    pick, wpack, wbuf, act, cotb, owbuf, qkv, att, lo_send, lo_recv, lo_mid, g_send, g_recv, g_mid,
    wx_s, wx_r, wy_s, wy_r, wf_s, ax_s, ax_r, cx_s, cx_r, oy_s, oy_r, of_s,
    lx_s, lx_r, gy_s, gy_r, gm_s, gm_r, in_s, z1_s, z1_r, z2_s, z2_r, yh_s, yh_r,
):
    r = lax.axis_index("replica")
    f = lax.axis_index("fsdp")
    x, y = f // NY, lax.rem(f, NY)
    pieces = lax.axis_size("replica") // 2
    own = r // 4 * 2 + lax.rem(r, 2)
    y_hi = lax.rem(r // 2, 2)

    loads = [
        pltpu.make_async_copy(src, dst, in_s.at[i])
        for i, (src, dst) in enumerate(
            [
                (qkvw_hbm, qkvw_ref), (patch_hbm, patch_ref), (outw_hbm, outw_ref), (cot_hbm, cot_ref),
                (delta_hbm, delta_ref), (mom_hbm, mom_ref), (par_hbm, par_ref),
            ]
        )
    ]
    for i in (0, 4, 1, 3, 2, 5, 6):
        loads[i].start()

    def at_x(k):
        return lax.rem(x + k, NX)

    def at_y(k):
        return lax.rem(y + k, NY)

    def dev_x(k):
        return (r, at_x(k) * NY + y)

    def dev_y(yy):
        return (r, x * NY + yy)

    def dev_p(k):
        to = lax.rem(own + k, pieces)
        return (to // 2 * 4 + y_hi * 2 + lax.rem(to, 2), f)

    def remote(src, dst, s, t, dev):
        return pltpu.make_async_remote_copy(
            src_ref=src, dst_ref=dst, send_sem=s, recv_sem=t, device_id=dev, device_id_type=MESH
        )

    barrier = pltpu.get_barrier_semaphore()
    partners = [dev_x(k) for k in (1, 2, 3)] + [dev_y(at_y(k)) for k in (1, 2, 3)]
    partners += [(r + 2 - 4 * y_hi, f)] + [dev_p(k) for k in range(1, pieces)]
    for dev in partners:
        pl.semaphore_signal(barrier, inc=1, device_id=dev, device_id_type=MESH)

    loads[0].wait()
    for k in range(NX):
        start = min(224 * k // 128, 4) * 128
        row = lax.broadcasted_iota(jnp.int32, (384, 256), 0)
        lane = lax.broadcasted_iota(jnp.int32, (384, 256), 1)
        wanted = 224 * k - start + 56 * (lane // 64) + lane % 64
        chosen = jnp.where((row == wanted) & (lane % 64 < 56), 1.0, 0.0).astype(BF16)
        for t in range(3):
            cols = qkvw_ref[:, 896 * t + start : 896 * t + start + 384]
            wpack[k, :, 256 * t : 256 * t + 256] = dot(cols, chosen).astype(BF16)
    wbuf[f] = wpack[x]

    def synced(ref):
        return jnp.where(jnp.full((256, 128), index_ref[0], jnp.int32) == 0, ref[:, 0, :], ref[:, 1, :])

    loads[4].wait()
    local[...] = synced(delta_ref)

    def rows_of(k):
        return pl.ds(pl.multiple_of(16 * lax.rem(own + k, pieces), 16), 16)

    def part_out(k):
        at = pieces - k
        return remote(local.at[rows_of(k)], parts.at[at], z1_s.at[k], z1_r.at[at], dev_p(k))

    def part_in(k):
        return remote(parts.at[k], parts.at[k], z1_s.at[pieces - k], z1_r.at[k], dev_p(k))

    def sum_out(k):
        mine = total.at[rows_of(0)]
        return remote(mine, mine, z2_s.at[k], z2_r.at[pieces - k], dev_p(k))

    def sum_in(k):
        theirs = total.at[rows_of(k)]
        return remote(theirs, theirs, z2_s.at[pieces - k], z2_r.at[k], dev_p(k))

    over_y = remote(piece, from_y, yh_s, yh_r, (r + 2 - 4 * y_hi, f))
    pl.semaphore_wait(barrier, len(partners))

    def w_x(k):
        return remote(wpack.at[at_x(k)], wbuf.at[f], wx_s.at[k], wx_r.at[NX - k], dev_x(k))

    def w_x_in(k):
        slot = wbuf.at[at_x(k) * NY + y]
        return remote(slot, slot, wx_s.at[NX - k], wx_r.at[k], dev_x(k))

    def along_y(buf, send, recv, fwd):
        def out(k):
            to = at_y(k)
            return remote(buf(y), buf(y), send(k), recv(y), dev_y(to))

        def near(k):
            return jnp.abs(at_y(k) - y) < 3

        def start():
            for k in (1, 3, 2):
                pl.when(near(k))(lambda k=k: out(k).start())

        def forward():
            def from_low():
                remote(buf(0), buf(0), fwd, recv(0), dev_y(3)).wait_recv()
                remote(buf(0), buf(0), fwd, recv(0), dev_y(3)).start()

            def from_high():
                remote(buf(3), buf(3), fwd, recv(3), dev_y(0)).wait_recv()
                remote(buf(3), buf(3), fwd, recv(3), dev_y(0)).start()

            pl.when(y == 2)(from_low)
            pl.when(y == 1)(from_high)

        def finish():
            for k in (1, 2, 3):
                src = at_y(k)
                done = ((y == 2) & (src == 0)) | ((y == 1) & (src == 3))
                pl.when(jnp.logical_not(done))(
                    lambda src=src: remote(buf(src), buf(src), fwd, recv(src), dev_y(src)).wait_recv()
                )

        def drain():
            for k in (1, 3, 2):
                pl.when(near(k))(lambda k=k: out(k).wait_send())
            pl.when((y == 1) | (y == 2))(
                lambda: remote(buf(y), buf(y), fwd, recv(y), dev_y(at_y(1))).wait_send()
            )

        return start, forward, finish, drain

    w_y = [
        along_y(
            lambda yy, k=k: wbuf.at[at_x(k) * NY + yy],
            lambda j, k=k: wy_s.at[k, j],
            lambda yy, k=k: wy_r.at[k, yy],
            wf_s.at[k],
        )
        for k in range(NX)
    ]
    o_y = along_y(lambda yy: owbuf.at[yy], lambda j: oy_s.at[j], lambda yy: oy_r.at[yy], of_s)

    for k in (2, 1, 3):
        w_x(k).start()
    w_y[0][0]()
    for k in range(1, pieces):
        part_out(k).start()

    mask = mask_ref[...]
    n = mask.shape[1]
    upper = (
        lax.broadcasted_iota(jnp.int32, (n, n), 0) <= lax.broadcasted_iota(jnp.int32, (n, n), 1)
    )
    place = dot(
        jnp.broadcast_to(mask, (16, n)).astype(F32).astype(BF16),
        jnp.where(upper, 1.0, 0.0).astype(BF16),
    )[0:1, :].astype(jnp.int32)
    place = jnp.where(mask > 0, place - 1, -1)
    pick[...] = jnp.where(
        lax.broadcasted_iota(jnp.int32, (ROWS, n), 0) == place, 1.0, 0.0
    ).astype(BF16)
    loads[1].wait()
    kept = dot(pick[...], patch_ref[...])
    shifted = kept - jnp.mean(kept, axis=-1, keepdims=True)
    spread = jnp.mean(shifted * shifted, axis=-1, keepdims=True)
    act[x] = (shifted * lax.rsqrt(spread + EPS)).astype(BF16)

    low, high = pl.ds(0, HALF), pl.ds(HALF, HALF)

    def along_x(buf, send, recv):
        def move(i, who, rows, to):
            return remote(buf.at[who, rows], buf.at[who, rows], send.at[i], recv.at[i], dev_x(to))

        def own():
            return [move(0, x, low, 1), move(1, x, high, 3), move(2, x, high, 1), move(3, x, low, 3)]

        def passing():
            return [move(4, at_x(3), low, 1), move(5, at_x(1), high, 3)]

        def incoming():
            return [
                move(0, at_x(3), low, 3), move(1, at_x(1), high, 1),
                move(2, at_x(3), high, 3), move(3, at_x(1), low, 1),
                move(4, at_x(2), low, 2), move(5, at_x(2), high, 2),
            ]

        def start():
            for c in own():
                c.start()

        def forward():
            got = incoming()
            for i in (0, 1):
                got[i].wait_recv()
                passing()[i].start()

        def finish():
            for c in incoming()[2:]:
                c.wait_recv()

        def drain():
            for c in own() + passing():
                c.wait_send()

        return start, forward, finish, drain

    a_x = along_x(act, ax_s, ax_r)
    c_x = along_x(cotb, cx_s, cx_r)
    a_x[0]()

    for k in (1, 3, 2):
        w_x_in(k).wait_recv()
        w_y[k][0]()

    loads[2].wait()
    owbuf[y, 0:56, :] = outw_ref[...]
    owbuf[y, 56:64, :] = jnp.zeros((8, outw_ref.shape[1]), BF16)
    loads[3].wait()
    cotb[x] = dot(pick[...], cot_ref[...]).astype(BF16)
    a_x[1]()
    c_x[0]()
    mine = local[rows_of(0), :]
    for k in range(1, pieces):
        part_in(k).wait_recv()
        mine = mine + parts[k]
    piece[...] = mine
    over_y.start()
    for k in (0, 1):
        w_y[k][1]()
    over_y.wait_recv()
    total[rows_of(0), :] = piece[...] + from_y[...]
    for k in range(1, pieces):
        sum_out(k).start()
    for k in (3, 2):
        w_y[k][1]()
    o_y[0]()
    c_x[1]()
    for k in range(1, pieces):
        sum_in(k).wait_recv()
    loads[5].wait()
    loads[6].wait()
    average = total[...] / lax.axis_size("replica")
    new_m = 0.9 * synced(mom_ref) + average
    newm_ref[...] = new_m
    newp_ref[...] = synced(par_ref) - 0.7 * (average + 0.9 * new_m)

    a_x[2]()
    for k in range(NX):
        w_y[k][2]()
    width = act.shape[2]
    qkv[...] = dot(
        act[...].reshape(NX * ROWS, width), wbuf[...].reshape(width, 768)
    ).astype(BF16).reshape(NX, ROWS, 768)

    def attend(i, carry):
        for h in range(2):
            q = qkv[i, :, 128 * h : 128 * h + 128]
            key = qkv[i, :, 256 + 128 * h : 384 + 128 * h]
            val = qkv[i, :, 512 + 128 * h : 640 + 128 * h]
            scores = dot(q, key, (((1,), (1,)), ((), ()))) * (1.0 / math.sqrt(HSZ))
            col = lax.broadcasted_iota(jnp.int32, (ROWS, ROWS), 1)
            scores = jnp.where(col < KEEP, scores, -1e30)
            expo = jnp.exp(scores - jnp.max(scores, axis=-1, keepdims=True))
            probs = (expo / jnp.sum(expo, axis=-1, keepdims=True)).astype(BF16)
            att[i, :, 128 * h : 128 * h + 128] = dot(probs, val).astype(BF16)
        return carry

    lax.fori_loop(0, NX, attend, 0)

    o_y[1]()
    o_y[2]()

    def project(k):
        lo_send[at_x(k)] = dot(att[at_x(k)], owbuf[...].reshape(NY * 64, width)).astype(BF16)

    def lo(i, src, dst, to):
        return remote(src, dst, lx_s.at[i], lx_r.at[i], dev_x(to))

    right, left, over = at_x(1), at_x(3), at_x(2)
    lo_far = [
        lo(0, lo_send.at[over, low], lo_mid.at[0], 1), lo(1, lo_send.at[over, high], lo_mid.at[1], 3)
    ]
    lo_own = [
        lo(2, lo_send.at[right, high], lo_recv.at[0, high], 1),
        lo(3, lo_send.at[left, low], lo_recv.at[1, low], 3),
    ]
    lo_both = [
        lo(4, lo_send.at[right, low], lo_recv.at[0, low], 1),
        lo(5, lo_send.at[left, high], lo_recv.at[1, high], 3),
    ]
    project(2)
    for c in lo_far:
        c.start()
    project(1)
    lo_own[0].start()
    project(3)
    lo_own[1].start()

    c_x[2]()
    g_send[...] = dot(
        att[...].reshape(NX * ROWS, 256), cotb[...].reshape(NX * ROWS, width), (((0,), (0,)), ((), ()))
    ).astype(BF16).reshape(NY, 64, width)

    def g(k):
        return remote(g_send.at[at_y(k)], g_recv.at[NY - k], gy_s.at[k], gy_r.at[NY - k], dev_y(at_y(k)))

    def g_in(k):
        return remote(g_recv.at[k], g_recv.at[k], gy_s.at[NY - k], gy_r.at[k], dev_y(at_y(k)))

    def g_far(to, via):
        return remote(g_send.at[to], g_mid, gm_s, gm_r, dev_y(via))

    ends = (y == 0) | (y == NY - 1)
    pl.when(y == 0)(lambda: g_far(3, 1).start())
    pl.when(y == 3)(lambda: g_far(0, 2).start())

    def near_y(k):
        return jnp.abs(at_y(k) - y) < 2

    for k in (1, 3):
        pl.when(near_y(k))(lambda k=k: g(k).start())
    pl.when(ends)(lambda: g(2).start())

    lo_far[0].wait_recv()
    lo_send[right, low] = (lo_send[right, low].astype(F32) + lo_mid[0].astype(F32)).astype(BF16)
    lo_both[0].start()
    lo_far[1].wait_recv()
    lo_send[left, high] = (lo_send[left, high].astype(F32) + lo_mid[1].astype(F32)).astype(BF16)
    lo_both[1].start()

    def g_pass():
        to = jnp.where(y == 1, 3, 0)
        g_far(0, 2).wait_recv()
        g_send[to] = (g_send[to].astype(F32) + g_mid[...].astype(F32)).astype(BF16)
        g(2).start()

    pl.when(jnp.logical_not(ends))(g_pass)
    project(0)

    whole = g_send[y].astype(F32)
    g_in(2).wait_recv()
    grad_ref[...] = (whole + g_recv[2].astype(F32))[0:56, :]
    for k in (1, 3):

        def add(k=k):
            g_in(k).wait_recv()
            grad_ref[...] += g_recv[k, 0:56].astype(F32)

        pl.when(near_y(k))(add)

    for i in (0, 1):
        lo_own[i].wait_recv()
    for i in (0, 1):
        lo_both[i].wait_recv()
    result = lo_send[x].astype(F32) + lo_recv[0].astype(F32) + lo_recv[1].astype(F32)
    out_ref[...] = dot(pick[...], result.astype(BF16), (((0,), (0,)), ((), ()))).astype(BF16)

    for k in (1, 2, 3):
        w_x(k).wait_send()
    for c in lo_far + lo_own + lo_both:
        c.wait_send()
    for k in range(1, pieces):
        part_out(k).wait_send()
        sum_out(k).wait_send()
    over_y.wait_send()
    for k in (1, 3):
        pl.when(near_y(k))(lambda k=k: g(k).wait_send())
    g(2).wait_send()
    pl.when(ends)(lambda: g_far(0, 1).wait_send())
    for k in range(NX):
        w_y[k][3]()
    o_y[3]()
    a_x[3]()
    c_x[3]()


def on_device(
    patch_rows, qkv_weight, out_weight, cotangent, keep_mask, outer_delta, momentum, global_params,
    fragment_index,
):
    def tiled(rows):
        return rows.reshape(2, 256, 128).transpose(1, 0, 2)

    pieces = lax.axis_size("replica") // 2
    width = patch_rows.shape[2]
    vmem = pl.BlockSpec(memory_space=pltpu.VMEM)
    hbm = pl.BlockSpec(memory_space=pltpu.HBM)
    sem = pltpu.SemaphoreType.DMA
    shapes = [
        jax.ShapeDtypeStruct((256, width), BF16),
        jax.ShapeDtypeStruct((56, width), F32),
        jax.ShapeDtypeStruct((256, 128), F32),
        jax.ShapeDtypeStruct((256, 128), F32),
    ]
    out, grad, new_m, new_p = pl.pallas_call(
        kernel,
        out_shape=shapes,
        in_specs=[hbm] * 7 + [vmem, pl.BlockSpec(memory_space=pltpu.SMEM)],
        out_specs=[vmem] * 4,
        scratch_shapes=[
            pltpu.VMEM((256, width), BF16),
            pltpu.VMEM((112, 2688), BF16),
            pltpu.VMEM((56, width), BF16),
            pltpu.VMEM((256, width), BF16),
            pltpu.VMEM((256, 2, 128), F32),
            pltpu.VMEM((256, 2, 128), F32),
            pltpu.VMEM((256, 2, 128), F32),
            pltpu.VMEM((256, 128), F32),
            pltpu.VMEM((16, 128), F32),
            pltpu.VMEM((16, 128), F32),
            pltpu.VMEM((pieces, 16, 128), F32),
            pltpu.VMEM((256, 128), F32),
            pltpu.VMEM((ROWS, 256), BF16),
            pltpu.VMEM((NX, 112, 768), BF16),
            pltpu.VMEM((NX * NY, 112, 768), BF16),
            pltpu.VMEM((NX, ROWS, width), BF16),
            pltpu.VMEM((NX, ROWS, width), BF16),
            pltpu.VMEM((NY, 64, width), BF16),
            pltpu.VMEM((NX, ROWS, 768), BF16),
            pltpu.VMEM((NX, ROWS, 256), BF16),
            pltpu.VMEM((NX, ROWS, width), BF16),
            pltpu.VMEM((2, ROWS, width), BF16),
            pltpu.VMEM((2, HALF, width), BF16),
            pltpu.VMEM((NY, 64, width), BF16),
            pltpu.VMEM((NY, 64, width), BF16),
            pltpu.VMEM((64, width), BF16),
            sem((NX,)), sem((NX,)),
            sem((NX, NY)), sem((NX, NY)), sem((NX,)),
            sem((6,)), sem((6,)), sem((6,)), sem((6,)),
            sem((NY,)), sem((NY,)), sem,
            sem((6,)), sem((6,)), sem((NY,)), sem((NY,)), sem, sem, sem((7,)),
            sem((pieces,)), sem((pieces,)), sem((pieces,)), sem((pieces,)), sem, sem,
        ],
        compiler_params=pltpu.CompilerParams(
            collective_id=0, has_side_effects=True, vmem_limit_bytes=63 * 1024 * 1024
        ),
        cost_estimate=pl.CostEstimate(flops=100_000_000_000, bytes_accessed=5_000_000, transcendentals=0),
    )(
        patch_rows[0], qkv_weight[0], out_weight[0], cotangent[0], tiled(outer_delta[0]),
        tiled(momentum), tiled(global_params), keep_mask, fragment_index,
    )
    return out[None], grad[None], new_m.reshape(-1), new_p.reshape(-1)


def solution(mesh):
    in_specs = (
        P(("replica", "fsdp"), None, None),
        P("replica", "fsdp", None),
        P("replica", "fsdp", None),
        P(("replica", "fsdp"), None, None),
        P(("replica", "fsdp"), None),
        P("replica", None, "fsdp"),
        P(None, "fsdp"),
        P(None, "fsdp"),
        P(),
    )
    out_specs = (
        P(("replica", "fsdp"), None, None),
        P("replica", "fsdp", None),
        P("fsdp"),
        P("fsdp"),
    )
    return jax.shard_map(
        on_device, mesh=mesh, in_specs=in_specs, out_specs=out_specs, check_vma=False
    )
```

```python
import math

import jax
import jax.numpy as jnp
from jax import lax
from jax.experimental import pallas as pl
from jax.experimental.pallas import tpu as pltpu
from jax.sharding import PartitionSpec as P

HSZ = 112
HEADS = 8
KEEP = 154
ROWS = 160
HALF = ROWS // 2
NX = 4
NY = 4
EPS = 1e-06
MESH = pl.DeviceIdType.MESH
F32 = jnp.float32
BF16 = jnp.bfloat16


def dot(a, b, dims=(((1,), (0,)), ((), ()))):
    return lax.dot_general(a, b, dims, preferred_element_type=F32)


def kernel(
    patch_hbm, qkvw_hbm, outw_hbm, cot_hbm, delta_hbm, mom_hbm, par_hbm, mask_ref, index_ref,
    out_ref, grad_ref, newm_ref, newp_ref,
    patch_ref, qkvw_ref, outw_ref, cot_ref, delta_ref, mom_ref, par_ref,
    local, piece, from_y, parts, total,
    pick, wide, wpack, wbuf, whole_w, act, cotb, oraw, owbuf, qkv, att, lo_send, lo_recv, lo_mid, g_send, g_recv, g_mid,
    wx_s, wx_r, wy_s, wy_r, wf_s, ax_s, ax_r, cx_s, cx_r, oy_s, oy_r, of_s,
    lx_s, lx_r, gy_s, gy_r, gm_s, gm_r, in_s, z1_s, z1_r, z2_s, z2_r, yh_s, yh_r,
):
    r = lax.axis_index("replica")
    f = lax.axis_index("fsdp")
    x, y = f // NY, lax.rem(f, NY)
    pieces = lax.axis_size("replica") // 2
    own = r // 4 * 2 + lax.rem(r, 2)
    y_hi = lax.rem(r // 2, 2)

    loads = [
        pltpu.make_async_copy(src, dst, in_s.at[i])
        for i, (src, dst) in enumerate(
            [
                (qkvw_hbm, qkvw_ref), (patch_hbm, patch_ref), (outw_hbm, outw_ref), (cot_hbm, cot_ref),
                (delta_hbm, delta_ref), (mom_hbm, mom_ref), (par_hbm, par_ref),
            ]
        )
    ]
    for i in (0, 4, 1, 3, 2, 5, 6):
        loads[i].start()

    def at_x(k):
        return lax.rem(x + k, NX)

    def at_y(k):
        return lax.rem(y + k, NY)

    def dev_x(k):
        return (r, at_x(k) * NY + y)

    def dev_y(yy):
        return (r, x * NY + yy)

    def dev_p(k):
        to = lax.rem(own + k, pieces)
        return (to // 2 * 4 + y_hi * 2 + lax.rem(to, 2), f)

    def remote(src, dst, s, t, dev):
        return pltpu.make_async_remote_copy(
            src_ref=src, dst_ref=dst, send_sem=s, recv_sem=t, device_id=dev, device_id_type=MESH
        )

    barrier = pltpu.get_barrier_semaphore()
    partners = [dev_x(k) for k in (1, 2, 3)] + [dev_y(at_y(k)) for k in (1, 2, 3)]
    partners += [(r + 2 - 4 * y_hi, f)] + [dev_p(k) for k in range(1, pieces)]
    for dev in partners:
        pl.semaphore_signal(barrier, inc=1, device_id=dev, device_id_type=MESH)

    def one_hot(shape, of):
        row = lax.broadcasted_iota(jnp.int32, shape, 0)
        return jnp.where(of(row, lax.broadcasted_iota(jnp.int32, shape, 1)), 1.0, 0.0).astype(BF16)

    loads[0].wait()
    for k in range(NX):
        start = min(224 * k // 128, 4) * 128
        shift = 224 * k - start
        chosen = one_hot(
            (384, 256), lambda i, j: (i == shift + 112 * (j // 128) + j % 128) & (j % 128 < 112)
        )
        for t in range(3):
            cols = qkvw_ref[:, 896 * t + start : 896 * t + start + 384]
            wide[112 * k : 112 * k + 112, 256 * t : 256 * t + 256] = dot(cols, chosen).astype(BF16)
    spread6 = one_hot(
        (128, 768),
        lambda i, j: ((j < 640) & (j % 128 >= 112) & (i == 16 * (j // 128) + j % 128 - 112))
        | ((j >= 640) & (i == 80 + j % 32)),
    )
    filled = dot(wide[:, 640:768], spread6)
    fold = one_hot((32, 112), lambda i, j: (i < 28) & (j % 28 == i))
    group = (
        lax.broadcasted_iota(jnp.int32, (112, 128), 0) // 28
        == lax.broadcasted_iota(jnp.int32, (112, 128), 1) // 32
    )
    for k in range(NX):
        rows = slice(112 * k, 112 * k + 112)
        for t in range(5):
            lanes = slice(128 * t, 128 * t + 128)
            wpack[k, 112 * t : 112 * t + 112, :] = (
                wide[rows, lanes].astype(F32) + filled[rows, lanes]
            ).astype(BF16)
        rest = jnp.where(group, filled[rows, 640:768], 0.0).astype(BF16)
        wpack[k, 560:592, :] = dot(fold, rest).astype(BF16)
    wbuf[f] = wpack[x]

    def synced(ref):
        return jnp.where(jnp.full((256, 128), index_ref[0], jnp.int32) == 0, ref[:, 0, :], ref[:, 1, :])

    loads[4].wait()
    local[...] = synced(delta_ref)

    def rows_of(k):
        return pl.ds(pl.multiple_of(16 * lax.rem(own + k, pieces), 16), 16)

    def part_out(k):
        at = pieces - k
        return remote(local.at[rows_of(k)], parts.at[at], z1_s.at[k], z1_r.at[at], dev_p(k))

    def part_in(k):
        return remote(parts.at[k], parts.at[k], z1_s.at[pieces - k], z1_r.at[k], dev_p(k))

    def sum_out(k):
        mine = total.at[rows_of(0)]
        return remote(mine, mine, z2_s.at[k], z2_r.at[pieces - k], dev_p(k))

    def sum_in(k):
        theirs = total.at[rows_of(k)]
        return remote(theirs, theirs, z2_s.at[pieces - k], z2_r.at[k], dev_p(k))

    over_y = remote(piece, from_y, yh_s, yh_r, (r + 2 - 4 * y_hi, f))
    pl.semaphore_wait(barrier, len(partners))

    def w_x(k):
        return remote(wpack.at[at_x(k)], wbuf.at[f], wx_s.at[k], wx_r.at[NX - k], dev_x(k))

    def w_x_in(k):
        slot = wbuf.at[at_x(k) * NY + y]
        return remote(slot, slot, wx_s.at[NX - k], wx_r.at[k], dev_x(k))

    def along_y(buf, send, recv, fwd):
        def out(k):
            to = at_y(k)
            return remote(buf(y), buf(y), send(k), recv(y), dev_y(to))

        def near(k):
            return jnp.abs(at_y(k) - y) < 3

        def start():
            for k in (1, 3, 2):
                pl.when(near(k))(lambda k=k: out(k).start())

        def forward():
            def from_low():
                remote(buf(0), buf(0), fwd, recv(0), dev_y(3)).wait_recv()
                remote(buf(0), buf(0), fwd, recv(0), dev_y(3)).start()

            def from_high():
                remote(buf(3), buf(3), fwd, recv(3), dev_y(0)).wait_recv()
                remote(buf(3), buf(3), fwd, recv(3), dev_y(0)).start()

            pl.when(y == 2)(from_low)
            pl.when(y == 1)(from_high)

        def finish():
            for k in (1, 2, 3):
                src = at_y(k)
                done = ((y == 2) & (src == 0)) | ((y == 1) & (src == 3))
                pl.when(jnp.logical_not(done))(
                    lambda src=src: remote(buf(src), buf(src), fwd, recv(src), dev_y(src)).wait_recv()
                )

        def drain():
            for k in (1, 3, 2):
                pl.when(near(k))(lambda k=k: out(k).wait_send())
            pl.when((y == 1) | (y == 2))(
                lambda: remote(buf(y), buf(y), fwd, recv(y), dev_y(at_y(1))).wait_send()
            )

        return start, forward, finish, drain

    w_y = [
        along_y(
            lambda yy, k=k: wbuf.at[at_x(k) * NY + yy],
            lambda j, k=k: wy_s.at[k, j],
            lambda yy, k=k: wy_r.at[k, yy],
            wf_s.at[k],
        )
        for k in range(NX)
    ]
    o_y = along_y(lambda yy: oraw.at[yy], lambda j: oy_s.at[j], lambda yy: oy_r.at[yy], of_s)

    for k in (2, 1, 3):
        w_x(k).start()
    w_y[0][0]()
    for k in range(1, pieces):
        part_out(k).start()

    mask = mask_ref[...]
    n = mask.shape[1]
    upper = (
        lax.broadcasted_iota(jnp.int32, (n, n), 0) <= lax.broadcasted_iota(jnp.int32, (n, n), 1)
    )
    place = dot(
        jnp.broadcast_to(mask, (16, n)).astype(F32).astype(BF16),
        jnp.where(upper, 1.0, 0.0).astype(BF16),
    )[0:1, :].astype(jnp.int32)
    place = jnp.where(mask > 0, place - 1, -1)
    pick[...] = jnp.where(
        lax.broadcasted_iota(jnp.int32, (ROWS, n), 0) == place, 1.0, 0.0
    ).astype(BF16)
    loads[1].wait()
    kept = dot(pick[...], patch_ref[...])
    shifted = kept - jnp.mean(kept, axis=-1, keepdims=True)
    spread = jnp.mean(shifted * shifted, axis=-1, keepdims=True)
    act[x] = (shifted * lax.rsqrt(spread + EPS)).astype(BF16)

    low, high = pl.ds(0, HALF), pl.ds(HALF, HALF)

    def along_x(buf, send, recv):
        def move(i, who, rows, to):
            return remote(buf.at[who, rows], buf.at[who, rows], send.at[i], recv.at[i], dev_x(to))

        def own():
            return [move(0, x, low, 1), move(1, x, high, 3), move(2, x, high, 1), move(3, x, low, 3)]

        def passing():
            return [move(4, at_x(3), low, 1), move(5, at_x(1), high, 3)]

        def incoming():
            return [
                move(0, at_x(3), low, 3), move(1, at_x(1), high, 1),
                move(2, at_x(3), high, 3), move(3, at_x(1), low, 1),
                move(4, at_x(2), low, 2), move(5, at_x(2), high, 2),
            ]

        def start():
            for c in own():
                c.start()

        def forward():
            got = incoming()
            for i in (0, 1):
                got[i].wait_recv()
                passing()[i].start()

        def finish():
            for c in incoming()[2:]:
                c.wait_recv()

        def drain():
            for c in own() + passing():
                c.wait_send()

        return start, forward, finish, drain

    a_x = along_x(act, ax_s, ax_r)
    c_x = along_x(cotb, cx_s, cx_r)
    a_x[0]()

    for k in (1, 3, 2):
        w_x_in(k).wait_recv()
        w_y[k][0]()

    loads[2].wait()
    oraw[y, 0:56, :] = outw_ref[:, 0:896]
    oraw[y, 56:112, :] = outw_ref[:, 896:1792]
    loads[3].wait()
    cotb[x] = dot(pick[...], cot_ref[...]).astype(BF16)
    a_x[1]()
    c_x[0]()
    mine = local[rows_of(0), :]
    for k in range(1, pieces):
        part_in(k).wait_recv()
        mine = mine + parts[k]
    piece[...] = mine
    over_y.start()
    for k in (0, 1):
        w_y[k][1]()
    over_y.wait_recv()
    total[rows_of(0), :] = piece[...] + from_y[...]
    for k in range(1, pieces):
        sum_out(k).start()
    for k in (3, 2):
        w_y[k][1]()
    o_y[0]()
    c_x[1]()
    for k in range(1, pieces):
        sum_in(k).wait_recv()
    loads[5].wait()
    loads[6].wait()
    average = total[...] / lax.axis_size("replica")
    new_m = 0.9 * synced(mom_ref) + average
    newm_ref[...] = new_m
    newp_ref[...] = synced(par_ref) - 0.7 * (average + 0.9 * new_m)

    a_x[2]()
    width = act.shape[2]
    unfold = one_hot((112, 32), lambda i, j: i % 28 == j)
    back = one_hot((128, 128), lambda i, j: (j < 32) & (i % 32 == j))

    for k in (0, 1, 3, 2):
        w_y[k][2]()

        def unpack(j, carry, k=k):
            at = at_x(k) * NY + j
            for t in range(5):
                whole_w[at, :, 128 * t : 128 * t + 128] = wbuf[at, 112 * t : 112 * t + 112, :]
            rest = jnp.where(group, dot(unfold, wbuf[at, 560:592, :]), 0.0).astype(BF16)
            whole_w[at, :, 640:768] = dot(rest, back).astype(BF16)
            return carry

        lax.fori_loop(0, NY, unpack, 0)
    qkv[...] = dot(
        act[...].reshape(NX * ROWS, width), whole_w[...].reshape(width, 768)
    ).astype(BF16).reshape(NX, ROWS, 768)
    sixth = one_hot(
        (768, 128),
        lambda i, j: ((i < 640) & (i % 128 >= 112) & (j == 16 * (i // 128) + i % 128 - 112))
        | ((i >= 640) & (i < 672) & (j == i - 560)),
    )

    def attend(i, carry):
        for h in range(2):
            q = qkv[i, :, 128 * h : 128 * h + 128]
            q = jnp.where(lax.broadcasted_iota(jnp.int32, (ROWS, 128), 1) < HSZ, q, jnp.zeros_like(q))
            key = qkv[i, :, 256 + 128 * h : 384 + 128 * h]
            val = qkv[i, :, 512:640] if h == 0 else dot(qkv[i], sixth).astype(BF16)
            scores = dot(q, key, (((1,), (1,)), ((), ()))) * (1.0 / math.sqrt(HSZ))
            col = lax.broadcasted_iota(jnp.int32, (ROWS, ROWS), 1)
            scores = jnp.where(col < KEEP, scores, -1e30)
            expo = jnp.exp(scores - jnp.max(scores, axis=-1, keepdims=True))
            probs = (expo / jnp.sum(expo, axis=-1, keepdims=True)).astype(BF16)
            att[i, :, 128 * h : 128 * h + 128] = dot(probs, val).astype(BF16)
        return carry

    lax.fori_loop(0, NX, attend, 0)

    o_y[1]()
    o_y[2]()
    for j in range(NY):
        rows = slice(128 * (j // 2) + 56 * (j % 2), 128 * (j // 2) + 56 * (j % 2) + 56)
        owbuf[rows, 0:896] = oraw[j, 0:56, :]
        owbuf[rows, 896:1792] = oraw[j, 56:112, :]
    for h in range(2):
        owbuf[128 * h + 112 : 128 * h + 128, :] = jnp.zeros((16, width), BF16)

    def project(k):
        lo_send[at_x(k)] = dot(att[at_x(k)], owbuf[...]).astype(BF16)

    def lo(i, src, dst, to):
        return remote(src, dst, lx_s.at[i], lx_r.at[i], dev_x(to))

    right, left, over = at_x(1), at_x(3), at_x(2)
    lo_far = [
        lo(0, lo_send.at[over, low], lo_mid.at[0], 1), lo(1, lo_send.at[over, high], lo_mid.at[1], 3)
    ]
    lo_own = [
        lo(2, lo_send.at[right, high], lo_recv.at[0, high], 1),
        lo(3, lo_send.at[left, low], lo_recv.at[1, low], 3),
    ]
    lo_both = [
        lo(4, lo_send.at[right, low], lo_recv.at[0, low], 1),
        lo(5, lo_send.at[left, high], lo_recv.at[1, high], 3),
    ]
    project(2)
    for c in lo_far:
        c.start()
    project(1)
    lo_own[0].start()
    project(3)
    lo_own[1].start()

    c_x[2]()
    terms = dot(
        att[...].reshape(NX * ROWS, 256), cotb[...].reshape(NX * ROWS, width), (((0,), (0,)), ((), ()))
    ).astype(BF16)
    for j in range(NY):
        rows = slice(128 * (j // 2) + 56 * (j % 2), 128 * (j // 2) + 56 * (j % 2) + 56)
        g_send[j, 0:56, :] = terms[rows, 0:896]
        g_send[j, 56:112, :] = terms[rows, 896:1792]

    def g(k):
        return remote(g_send.at[at_y(k)], g_recv.at[NY - k], gy_s.at[k], gy_r.at[NY - k], dev_y(at_y(k)))

    def g_in(k):
        return remote(g_recv.at[k], g_recv.at[k], gy_s.at[NY - k], gy_r.at[k], dev_y(at_y(k)))

    def g_far(to, via):
        return remote(g_send.at[to], g_mid, gm_s, gm_r, dev_y(via))

    ends = (y == 0) | (y == NY - 1)
    pl.when(y == 0)(lambda: g_far(3, 1).start())
    pl.when(y == 3)(lambda: g_far(0, 2).start())

    def near_y(k):
        return jnp.abs(at_y(k) - y) < 2

    for k in (1, 3):
        pl.when(near_y(k))(lambda k=k: g(k).start())
    pl.when(ends)(lambda: g(2).start())

    lo_far[0].wait_recv()
    lo_send[right, low] = (lo_send[right, low].astype(F32) + lo_mid[0].astype(F32)).astype(BF16)
    lo_both[0].start()
    lo_far[1].wait_recv()
    lo_send[left, high] = (lo_send[left, high].astype(F32) + lo_mid[1].astype(F32)).astype(BF16)
    lo_both[1].start()

    def g_pass():
        to = jnp.where(y == 1, 3, 0)
        g_far(0, 2).wait_recv()
        g_send[to] = (g_send[to].astype(F32) + g_mid[...].astype(F32)).astype(BF16)
        g(2).start()

    pl.when(jnp.logical_not(ends))(g_pass)
    project(0)

    whole = g_send[y].astype(F32)
    g_in(2).wait_recv()
    whole = whole + g_recv[2].astype(F32)
    grad_ref[:, 0:896] = whole[0:56, :]
    grad_ref[:, 896:1792] = whole[56:112, :]
    for k in (1, 3):

        def add(k=k):
            g_in(k).wait_recv()
            grad_ref[:, 0:896] += g_recv[k, 0:56].astype(F32)
            grad_ref[:, 896:1792] += g_recv[k, 56:112].astype(F32)

        pl.when(near_y(k))(add)

    for i in (0, 1):
        lo_own[i].wait_recv()
    for i in (0, 1):
        lo_both[i].wait_recv()
    result = lo_send[x].astype(F32) + lo_recv[0].astype(F32) + lo_recv[1].astype(F32)
    out_ref[...] = dot(pick[...], result.astype(BF16), (((0,), (0,)), ((), ()))).astype(BF16)

    for k in (1, 2, 3):
        w_x(k).wait_send()
    for c in lo_far + lo_own + lo_both:
        c.wait_send()
    for k in range(1, pieces):
        part_out(k).wait_send()
        sum_out(k).wait_send()
    over_y.wait_send()
    for k in (1, 3):
        pl.when(near_y(k))(lambda k=k: g(k).wait_send())
    g(2).wait_send()
    pl.when(ends)(lambda: g_far(0, 1).wait_send())
    for k in range(NX):
        w_y[k][3]()
    o_y[3]()
    a_x[3]()
    c_x[3]()


def hand_out(out_in, grad_in, newm_in, newp_in, out_ref, grad_ref, newm_ref, newp_ref, out_v, grad_v, m_v, p_v, sems):
    steps = [(out_in, out_v, out_ref, pl.ds(64 * i, 64)) for i in range(4)]
    steps += [(grad_in, grad_v, grad_ref, pl.ds(0, 56))]
    steps += [(newm_in, m_v, newm_ref, pl.ds(0, 256)), (newp_in, p_v, newp_ref, pl.ds(0, 256))]
    loads, stores = [], []
    for i, (src, held, dst, rows) in enumerate(steps):
        loads.append(pltpu.make_async_copy(src.at[rows], held.at[rows], sems.at[0, i]))
        stores.append(pltpu.make_async_copy(held.at[rows], dst.at[rows], sems.at[1, i]))
    for c in loads:
        c.start()
    for load, store in zip(loads, stores):
        load.wait()
        store.start()
    for c in stores:
        c.wait()


def on_device(
    patch_rows, qkv_weight, out_weight, cotangent, keep_mask, outer_delta, momentum, global_params,
    fragment_index,
):
    def tiled(rows):
        return rows.reshape(2, 256, 128).transpose(1, 0, 2)

    pieces = lax.axis_size("replica") // 2
    width = patch_rows.shape[2]
    vmem = pl.BlockSpec(memory_space=pltpu.VMEM)
    hbm = pl.BlockSpec(memory_space=pltpu.HBM)
    sem = pltpu.SemaphoreType.DMA
    shapes = [
        jax.ShapeDtypeStruct((256, width), BF16),
        jax.ShapeDtypeStruct((56, width), F32),
        jax.ShapeDtypeStruct((256, 128), F32),
        jax.ShapeDtypeStruct((256, 128), F32),
    ]
    results = pl.pallas_call(
        kernel,
        out_shape=shapes,
        in_specs=[hbm] * 7 + [vmem, pl.BlockSpec(memory_space=pltpu.SMEM)],
        out_specs=[vmem] * 4,
        scratch_shapes=[
            pltpu.VMEM((256, width), BF16),
            pltpu.VMEM((112, 2688), BF16),
            pltpu.VMEM((56, width), BF16),
            pltpu.VMEM((256, width), BF16),
            pltpu.VMEM((256, 2, 128), F32),
            pltpu.VMEM((256, 2, 128), F32),
            pltpu.VMEM((256, 2, 128), F32),
            pltpu.VMEM((256, 128), F32),
            pltpu.VMEM((16, 128), F32),
            pltpu.VMEM((16, 128), F32),
            pltpu.VMEM((pieces, 16, 128), F32),
            pltpu.VMEM((256, 128), F32),
            pltpu.VMEM((ROWS, 256), BF16),
            pltpu.VMEM((NX * 112, 768), BF16),
            pltpu.VMEM((NX, 592, 128), BF16),
            pltpu.VMEM((NX * NY, 592, 128), BF16),
            pltpu.VMEM((NX * NY, 112, 768), BF16),
            pltpu.VMEM((NX, ROWS, width), BF16),
            pltpu.VMEM((NX, ROWS, width), BF16),
            pltpu.VMEM((NY, 112, 896), BF16),
            pltpu.VMEM((256, width), BF16),
            pltpu.VMEM((NX, ROWS, 768), BF16),
            pltpu.VMEM((NX, ROWS, 256), BF16),
            pltpu.VMEM((NX, ROWS, width), BF16),
            pltpu.VMEM((2, ROWS, width), BF16),
            pltpu.VMEM((2, HALF, width), BF16),
            pltpu.VMEM((NY, 112, 896), BF16),
            pltpu.VMEM((NY, 112, 896), BF16),
            pltpu.VMEM((112, 896), BF16),
            sem((NX,)), sem((NX,)),
            sem((NX, NY)), sem((NX, NY)), sem((NX,)),
            sem((6,)), sem((6,)), sem((6,)), sem((6,)),
            sem((NY,)), sem((NY,)), sem,
            sem((6,)), sem((6,)), sem((NY,)), sem((NY,)), sem, sem, sem((7,)),
            sem((pieces,)), sem((pieces,)), sem((pieces,)), sem((pieces,)), sem, sem,
        ],
        compiler_params=pltpu.CompilerParams(
            collective_id=0, has_side_effects=True, vmem_limit_bytes=63 * 1024 * 1024
        ),
        cost_estimate=pl.CostEstimate(flops=100_000_000_000, bytes_accessed=5_000_000, transcendentals=0),
    )(
        patch_rows[0], qkv_weight[0], out_weight[0], cotangent[0], tiled(outer_delta[0]),
        tiled(momentum), tiled(global_params), keep_mask, fragment_index,
    )
    out, grad, new_m, new_p = pl.pallas_call(
        hand_out,
        out_shape=shapes,
        in_specs=[hbm] * 4,
        out_specs=[hbm] * 4,
        scratch_shapes=[pltpu.VMEM(a.shape, a.dtype) for a in shapes] + [sem((2, 7))],
        compiler_params=pltpu.CompilerParams(vmem_limit_bytes=63 * 1024 * 1024),
    )(*results)
    return out[None], grad[None], new_m.reshape(-1), new_p.reshape(-1)


def solution(mesh):
    in_specs = (
        P(("replica", "fsdp"), None, None),
        P("replica", "fsdp", None),
        P("replica", "fsdp", None),
        P(("replica", "fsdp"), None, None),
        P(("replica", "fsdp"), None),
        P("replica", None, "fsdp"),
        P(None, "fsdp"),
        P(None, "fsdp"),
        P(),
    )
    out_specs = (
        P(("replica", "fsdp"), None, None),
        P("replica", "fsdp", None),
        P("fsdp"),
        P("fsdp"),
    )
    return jax.shard_map(
        on_device, mesh=mesh, in_specs=in_specs, out_specs=out_specs, check_vma=False
    )
```

```python
import math

import jax
import jax.numpy as jnp
from jax import lax
from jax.experimental import pallas as pl
from jax.experimental.pallas import tpu as pltpu
from jax.sharding import PartitionSpec as P

HSZ = 112
HEADS = 8
KEEP = 154
ROWS = 160
HALF = ROWS // 2
NX = 4
NY = 4
EPS = 1e-06
MESH = pl.DeviceIdType.MESH
F32 = jnp.float32
BF16 = jnp.bfloat16


def dot(a, b, dims=(((1,), (0,)), ((), ()))):
    return lax.dot_general(a, b, dims, preferred_element_type=F32)


def kernel(
    patch_hbm, qkvw_hbm, outw_hbm, cot_hbm, delta_hbm, mom_hbm, par_hbm, mask_ref, index_ref,
    out_ref, grad_ref, newm_ref, newp_ref,
    patch_ref, qkvw_ref, outw_ref, cot_ref, delta_ref, mom_ref, par_ref,
    local, piece, from_y, parts, total,
    pick, wide, wpack, wbuf, whole_w, act, cotb, oraw, owbuf, qkv, att, lo_send, lo_recv, lo_mid, g_send, g_recv, g_mid,
    wx_s, wx_r, wy_s, wy_r, wf_s, ax_s, ax_r, cx_s, cx_r, oy_s, oy_r, of_s,
    lx_s, lx_r, gy_s, gy_r, gm_s, gm_r, in_s, z1_s, z1_r, z2_s, z2_r, yh_s, yh_r, below, above,
):
    r = lax.axis_index("replica")
    f = lax.axis_index("fsdp")
    x, y = f // NY, lax.rem(f, NY)
    pieces = lax.axis_size("replica") // 2
    own = r // 4 * 2 + lax.rem(r, 2)
    y_hi = lax.rem(r // 2, 2)
    z, nz = r // 4, lax.axis_size("replica") // 4

    loads = [
        pltpu.make_async_copy(src, dst, in_s.at[i])
        for i, (src, dst) in enumerate(
            [
                (qkvw_hbm, qkvw_ref), (patch_hbm, patch_ref), (outw_hbm, outw_ref), (cot_hbm, cot_ref),
                (delta_hbm, delta_ref), (mom_hbm, mom_ref), (par_hbm, par_ref),
            ]
        )
    ]
    for i in (0, 4, 1, 3, 2, 5, 6):
        loads[i].start()

    def at_x(k):
        return lax.rem(x + k, NX)

    def at_y(k):
        return lax.rem(y + k, NY)

    def dev_x(k):
        return (r, at_x(k) * NY + y)

    def dev_y(yy):
        return (r, x * NY + yy)

    def dev_p(k):
        to = lax.rem(own + k, pieces)
        return (to // 2 * 4 + y_hi * 2 + lax.rem(to, 2), f)

    def remote(src, dst, s, t, dev):
        return pltpu.make_async_remote_copy(
            src_ref=src, dst_ref=dst, send_sem=s, recv_sem=t, device_id=dev, device_id_type=MESH
        )

    barrier = pltpu.get_barrier_semaphore()
    partners = [dev_x(k) for k in (1, 2, 3)] + [dev_y(at_y(k)) for k in (1, 2, 3)]
    partners += [(r + 2 - 4 * y_hi, f), (r + 1 - 2 * lax.rem(r, 2), f)]
    for dev in partners:
        pl.semaphore_signal(barrier, inc=1, device_id=dev, device_id_type=MESH)

    def tell(sem, dev):
        pl.semaphore_signal(sem, inc=1, device_id=dev, device_id_type=MESH)

    pl.when(z > 0)(lambda: tell(barrier, (r - 4, f)))
    pl.when(z < nz - 1)(lambda: tell(barrier, (r + 4, f)))

    def from_below():
        pl.when(z > 0)(lambda: pl.semaphore_wait(below, 1))
        pl.when(z < nz - 1)(lambda: tell(below, (r + 4, f)))

    def from_above(p):
        def step():
            if p > 0:
                pl.semaphore_wait(above, 1)
            if p < nz - 1:
                tell(above, (r - 4, f))

        pl.when(z == nz - 1 - p)(step)

    def one_hot(shape, of):
        row = lax.broadcasted_iota(jnp.int32, shape, 0)
        return jnp.where(of(row, lax.broadcasted_iota(jnp.int32, shape, 1)), 1.0, 0.0).astype(BF16)

    loads[0].wait()
    for k in range(NX):
        start = min(224 * k // 128, 4) * 128
        shift = 224 * k - start
        chosen = one_hot(
            (384, 256), lambda i, j: (i == shift + 112 * (j // 128) + j % 128) & (j % 128 < 112)
        )
        for t in range(3):
            cols = qkvw_ref[:, 896 * t + start : 896 * t + start + 384]
            wide[112 * k : 112 * k + 112, 256 * t : 256 * t + 256] = dot(cols, chosen).astype(BF16)
    spread6 = one_hot(
        (128, 768),
        lambda i, j: ((j < 640) & (j % 128 >= 112) & (i == 16 * (j // 128) + j % 128 - 112))
        | ((j >= 640) & (i == 80 + j % 32)),
    )
    filled = dot(wide[:, 640:768], spread6)
    fold = one_hot((32, 112), lambda i, j: (i < 28) & (j % 28 == i))
    group = (
        lax.broadcasted_iota(jnp.int32, (112, 128), 0) // 28
        == lax.broadcasted_iota(jnp.int32, (112, 128), 1) // 32
    )
    for k in range(NX):
        rows = slice(112 * k, 112 * k + 112)
        for t in range(5):
            lanes = slice(128 * t, 128 * t + 128)
            wpack[k, 112 * t : 112 * t + 112, :] = (
                wide[rows, lanes].astype(F32) + filled[rows, lanes]
            ).astype(BF16)
        rest = jnp.where(group, filled[rows, 640:768], 0.0).astype(BF16)
        wpack[k, 560:592, :] = dot(fold, rest).astype(BF16)
    wbuf[f] = wpack[x]

    def synced(ref):
        return jnp.where(jnp.full((256, 128), index_ref[0], jnp.int32) == 0, ref[:, 0, :], ref[:, 1, :])


    def rows_of(k):
        return pl.ds(pl.multiple_of(16 * lax.rem(own + k, pieces), 16), 16)

    def part_out(k):
        at = pieces - k
        return remote(local.at[rows_of(k)], parts.at[at], z1_s.at[k], z1_r.at[at], dev_p(k))

    def part_in(k):
        return remote(parts.at[k], parts.at[k], z1_s.at[pieces - k], z1_r.at[k], dev_p(k))

    def sum_out(k):
        mine = total.at[rows_of(0)]
        return remote(mine, mine, z2_s.at[k], z2_r.at[pieces - k], dev_p(k))

    def sum_in(k):
        theirs = total.at[rows_of(k)]
        return remote(theirs, theirs, z2_s.at[pieces - k], z2_r.at[k], dev_p(k))

    over_y = remote(piece, from_y, yh_s, yh_r, (r + 2 - 4 * y_hi, f))
    beside = jnp.where((z > 0) & (z < nz - 1), 2, 1)
    pl.semaphore_wait(barrier, len(partners) + beside)
    from_below()
    from_above(0)

    def w_x(k):
        return remote(wpack.at[at_x(k)], wbuf.at[f], wx_s.at[k], wx_r.at[NX - k], dev_x(k))

    def w_x_in(k):
        slot = wbuf.at[at_x(k) * NY + y]
        return remote(slot, slot, wx_s.at[NX - k], wx_r.at[k], dev_x(k))

    def along_y(buf, send, recv, fwd):
        def out(k):
            to = at_y(k)
            return remote(buf(y), buf(y), send(k), recv(y), dev_y(to))

        def near(k):
            return jnp.abs(at_y(k) - y) < 3

        def start():
            for k in (1, 3, 2):
                pl.when(near(k))(lambda k=k: out(k).start())

        def forward():
            def from_low():
                remote(buf(0), buf(0), fwd, recv(0), dev_y(3)).wait_recv()
                remote(buf(0), buf(0), fwd, recv(0), dev_y(3)).start()

            def from_high():
                remote(buf(3), buf(3), fwd, recv(3), dev_y(0)).wait_recv()
                remote(buf(3), buf(3), fwd, recv(3), dev_y(0)).start()

            pl.when(y == 2)(from_low)
            pl.when(y == 1)(from_high)

        def finish():
            for k in (1, 2, 3):
                src = at_y(k)
                done = ((y == 2) & (src == 0)) | ((y == 1) & (src == 3))
                pl.when(jnp.logical_not(done))(
                    lambda src=src: remote(buf(src), buf(src), fwd, recv(src), dev_y(src)).wait_recv()
                )

        def drain():
            for k in (1, 3, 2):
                pl.when(near(k))(lambda k=k: out(k).wait_send())
            pl.when((y == 1) | (y == 2))(
                lambda: remote(buf(y), buf(y), fwd, recv(y), dev_y(at_y(1))).wait_send()
            )

        return start, forward, finish, drain

    w_y = [
        along_y(
            lambda yy, k=k: wbuf.at[at_x(k) * NY + yy],
            lambda j, k=k: wy_s.at[k, j],
            lambda yy, k=k: wy_r.at[k, yy],
            wf_s.at[k],
        )
        for k in range(NX)
    ]
    o_y = along_y(lambda yy: oraw.at[yy], lambda j: oy_s.at[j], lambda yy: oy_r.at[yy], of_s)

    for k in (2, 1, 3):
        w_x(k).start()
    w_y[0][0]()
    from_above(1)

    mask = mask_ref[...]
    n = mask.shape[1]
    upper = (
        lax.broadcasted_iota(jnp.int32, (n, n), 0) <= lax.broadcasted_iota(jnp.int32, (n, n), 1)
    )
    place = dot(
        jnp.broadcast_to(mask, (16, n)).astype(F32).astype(BF16),
        jnp.where(upper, 1.0, 0.0).astype(BF16),
    )[0:1, :].astype(jnp.int32)
    place = jnp.where(mask > 0, place - 1, -1)
    pick[...] = jnp.where(
        lax.broadcasted_iota(jnp.int32, (ROWS, n), 0) == place, 1.0, 0.0
    ).astype(BF16)
    loads[1].wait()
    kept = dot(pick[...], patch_ref[...])
    shifted = kept - jnp.mean(kept, axis=-1, keepdims=True)
    spread = jnp.mean(shifted * shifted, axis=-1, keepdims=True)
    act[x] = (shifted * lax.rsqrt(spread + EPS)).astype(BF16)

    low, high = pl.ds(0, HALF), pl.ds(HALF, HALF)

    def along_x(buf, send, recv):
        def move(i, who, rows, to):
            return remote(buf.at[who, rows], buf.at[who, rows], send.at[i], recv.at[i], dev_x(to))

        def own():
            return [move(0, x, low, 1), move(1, x, high, 3), move(2, x, high, 1), move(3, x, low, 3)]

        def passing():
            return [move(4, at_x(3), low, 1), move(5, at_x(1), high, 3)]

        def incoming():
            return [
                move(0, at_x(3), low, 3), move(1, at_x(1), high, 1),
                move(2, at_x(3), high, 3), move(3, at_x(1), low, 1),
                move(4, at_x(2), low, 2), move(5, at_x(2), high, 2),
            ]

        def start():
            for c in own():
                c.start()

        def forward():
            got = incoming()
            for i in (0, 1):
                got[i].wait_recv()
                passing()[i].start()

        def finish():
            for c in incoming()[2:]:
                c.wait_recv()

        def drain():
            for c in own() + passing():
                c.wait_send()

        return start, forward, finish, drain

    a_x = along_x(act, ax_s, ax_r)
    c_x = along_x(cotb, cx_s, cx_r)
    a_x[0]()
    from_above(2)

    for p, k in enumerate((1, 3, 2)):
        w_x_in(k).wait_recv()
        w_y[k][0]()
        from_above(3 + p)

    loads[2].wait()
    oraw[y, 0:56, :] = outw_ref[:, 0:896]
    oraw[y, 56:112, :] = outw_ref[:, 896:1792]
    loads[3].wait()
    cotb[x] = dot(pick[...], cot_ref[...]).astype(BF16)
    loads[4].wait()
    local[...] = synced(delta_ref)
    a_x[1]()
    c_x[0]()
    from_above(6)
    w_y[0][1]()
    for p in range(7, nz):
        from_above(p)
    for k in range(1, pieces):
        part_out(k).start()
    for k in (1, 3):
        w_y[k][1]()
    o_y[0]()
    mine = local[rows_of(0), :]
    for k in range(1, pieces):
        part_in(k).wait_recv()
        mine = mine + parts[k]
    piece[...] = mine
    over_y.start()
    w_y[2][1]()
    c_x[1]()
    over_y.wait_recv()
    total[rows_of(0), :] = piece[...] + from_y[...]
    for k in range(1, pieces):
        sum_out(k).start()
    o_y[1]()

    a_x[2]()
    width = act.shape[2]
    unfold = one_hot((112, 32), lambda i, j: i % 28 == j)
    back = one_hot((128, 128), lambda i, j: (j < 32) & (i % 32 == j))

    for k in (0, 1, 3, 2):
        w_y[k][2]()

        def unpack(j, carry, k=k):
            at = at_x(k) * NY + j
            for t in range(5):
                whole_w[at, :, 128 * t : 128 * t + 128] = wbuf[at, 112 * t : 112 * t + 112, :]
            rest = jnp.where(group, dot(unfold, wbuf[at, 560:592, :]), 0.0).astype(BF16)
            whole_w[at, :, 640:768] = dot(rest, back).astype(BF16)
            return carry

        lax.fori_loop(0, NY, unpack, 0)
    qkv[...] = dot(
        act[...].reshape(NX * ROWS, width), whole_w[...].reshape(width, 768)
    ).astype(BF16).reshape(NX, ROWS, 768)
    sixth = one_hot(
        (768, 128),
        lambda i, j: ((i < 640) & (i % 128 >= 112) & (j == 16 * (i // 128) + i % 128 - 112))
        | ((i >= 640) & (i < 672) & (j == i - 560)),
    )

    def attend(i):
        for h in range(2):
            q = qkv[i, :, 128 * h : 128 * h + 128]
            q = jnp.where(lax.broadcasted_iota(jnp.int32, (ROWS, 128), 1) < HSZ, q, jnp.zeros_like(q))
            key = qkv[i, :, 256 + 128 * h : 384 + 128 * h]
            val = qkv[i, :, 512:640] if h == 0 else dot(qkv[i], sixth).astype(BF16)
            scores = dot(q, key, (((1,), (1,)), ((), ()))) * (1.0 / math.sqrt(HSZ))
            col = lax.broadcasted_iota(jnp.int32, (ROWS, ROWS), 1)
            scores = jnp.where(col < KEEP, scores, -1e30)
            expo = jnp.exp(scores - jnp.max(scores, axis=-1, keepdims=True))
            probs = (expo / jnp.sum(expo, axis=-1, keepdims=True)).astype(BF16)
            att[i, :, 128 * h : 128 * h + 128] = dot(probs, val).astype(BF16)

    o_y[2]()
    for j in range(NY):
        rows = slice(128 * (j // 2) + 56 * (j % 2), 128 * (j // 2) + 56 * (j % 2) + 56)
        owbuf[rows, 0:896] = oraw[j, 0:56, :]
        owbuf[rows, 896:1792] = oraw[j, 56:112, :]
    for h in range(2):
        owbuf[128 * h + 112 : 128 * h + 128, :] = jnp.zeros((16, width), BF16)

    def project(k):
        lo_send[at_x(k)] = dot(att[at_x(k)], owbuf[...]).astype(BF16)

    def lo(i, src, dst, to):
        return remote(src, dst, lx_s.at[i], lx_r.at[i], dev_x(to))

    right, left, over = at_x(1), at_x(3), at_x(2)
    lo_far = [
        lo(0, lo_send.at[over, low], lo_mid.at[0], 1), lo(1, lo_send.at[over, high], lo_mid.at[1], 3)
    ]
    lo_own = [
        lo(2, lo_send.at[right, high], lo_recv.at[0, high], 1),
        lo(3, lo_send.at[left, low], lo_recv.at[1, low], 3),
    ]
    lo_both = [
        lo(4, lo_send.at[right, low], lo_recv.at[0, low], 1),
        lo(5, lo_send.at[left, high], lo_recv.at[1, high], 3),
    ]
    attend(over)
    project(2)
    for c in lo_far:
        c.start()
    attend(right)
    project(1)
    lo_own[0].start()
    attend(left)
    project(3)
    lo_own[1].start()
    attend(x)

    c_x[2]()
    terms = dot(
        att[...].reshape(NX * ROWS, 256), cotb[...].reshape(NX * ROWS, width), (((0,), (0,)), ((), ()))
    ).astype(BF16)
    for j in range(NY):
        rows = slice(128 * (j // 2) + 56 * (j % 2), 128 * (j // 2) + 56 * (j % 2) + 56)
        g_send[j, 0:56, :] = terms[rows, 0:896]
        g_send[j, 56:112, :] = terms[rows, 896:1792]

    def g(k):
        return remote(g_send.at[at_y(k)], g_recv.at[NY - k], gy_s.at[k], gy_r.at[NY - k], dev_y(at_y(k)))

    def g_in(k):
        return remote(g_recv.at[k], g_recv.at[k], gy_s.at[NY - k], gy_r.at[k], dev_y(at_y(k)))

    def g_far(to, via):
        return remote(g_send.at[to], g_mid, gm_s, gm_r, dev_y(via))

    ends = (y == 0) | (y == NY - 1)
    pl.when(y == 0)(lambda: g_far(3, 1).start())
    pl.when(y == 3)(lambda: g_far(0, 2).start())

    def near_y(k):
        return jnp.abs(at_y(k) - y) < 2

    for k in (1, 3):
        pl.when(near_y(k))(lambda k=k: g(k).start())
    pl.when(ends)(lambda: g(2).start())

    lo_far[0].wait_recv()
    lo_send[right, low] = (lo_send[right, low].astype(F32) + lo_mid[0].astype(F32)).astype(BF16)
    lo_both[0].start()
    lo_far[1].wait_recv()
    lo_send[left, high] = (lo_send[left, high].astype(F32) + lo_mid[1].astype(F32)).astype(BF16)
    lo_both[1].start()

    def g_pass():
        to = jnp.where(y == 1, 3, 0)
        g_far(0, 2).wait_recv()
        g_send[to] = (g_send[to].astype(F32) + g_mid[...].astype(F32)).astype(BF16)
        g(2).start()

    pl.when(jnp.logical_not(ends))(g_pass)
    project(0)

    for k in range(1, pieces):
        sum_in(k).wait_recv()
    loads[5].wait()
    loads[6].wait()
    average = total[...] / lax.axis_size("replica")
    new_m = 0.9 * synced(mom_ref) + average
    newm_ref[...] = new_m
    newp_ref[...] = synced(par_ref) - 0.7 * (average + 0.9 * new_m)

    whole = g_send[y].astype(F32)
    g_in(2).wait_recv()
    whole = whole + g_recv[2].astype(F32)
    grad_ref[:, 0:896] = whole[0:56, :]
    grad_ref[:, 896:1792] = whole[56:112, :]
    for k in (1, 3):

        def add(k=k):
            g_in(k).wait_recv()
            grad_ref[:, 0:896] += g_recv[k, 0:56].astype(F32)
            grad_ref[:, 896:1792] += g_recv[k, 56:112].astype(F32)

        pl.when(near_y(k))(add)

    for i in (0, 1):
        lo_own[i].wait_recv()
    for i in (0, 1):
        lo_both[i].wait_recv()
    result = lo_send[x].astype(F32) + lo_recv[0].astype(F32) + lo_recv[1].astype(F32)
    out_ref[...] = dot(pick[...], result.astype(BF16), (((0,), (0,)), ((), ()))).astype(BF16)

    for k in (1, 2, 3):
        w_x(k).wait_send()
    for c in lo_far + lo_own + lo_both:
        c.wait_send()
    for k in range(1, pieces):
        part_out(k).wait_send()
        sum_out(k).wait_send()
    over_y.wait_send()
    for k in (1, 3):
        pl.when(near_y(k))(lambda k=k: g(k).wait_send())
    g(2).wait_send()
    pl.when(ends)(lambda: g_far(0, 1).wait_send())
    for k in range(NX):
        w_y[k][3]()
    o_y[3]()
    a_x[3]()
    c_x[3]()


def hand_out(out_in, grad_in, newm_in, newp_in, out_ref, grad_ref, newm_ref, newp_ref, out_v, grad_v, m_v, p_v, sems):
    steps = [(out_in, out_v, out_ref, pl.ds(64 * i, 64)) for i in range(4)]
    steps += [(grad_in, grad_v, grad_ref, pl.ds(0, 56))]
    steps += [(newm_in, m_v, newm_ref, pl.ds(0, 256)), (newp_in, p_v, newp_ref, pl.ds(0, 256))]
    loads, stores = [], []
    for i, (src, held, dst, rows) in enumerate(steps):
        loads.append(pltpu.make_async_copy(src.at[rows], held.at[rows], sems.at[0, i]))
        stores.append(pltpu.make_async_copy(held.at[rows], dst.at[rows], sems.at[1, i]))
    for c in loads:
        c.start()
    for load, store in zip(loads, stores):
        load.wait()
        store.start()
    for c in stores:
        c.wait()


def on_device(
    patch_rows, qkv_weight, out_weight, cotangent, keep_mask, outer_delta, momentum, global_params,
    fragment_index,
):
    def tiled(rows):
        return rows.reshape(2, 256, 128).transpose(1, 0, 2)

    pieces = lax.axis_size("replica") // 2
    width = patch_rows.shape[2]
    vmem = pl.BlockSpec(memory_space=pltpu.VMEM)
    hbm = pl.BlockSpec(memory_space=pltpu.HBM)
    sem = pltpu.SemaphoreType.DMA
    shapes = [
        jax.ShapeDtypeStruct((256, width), BF16),
        jax.ShapeDtypeStruct((56, width), F32),
        jax.ShapeDtypeStruct((256, 128), F32),
        jax.ShapeDtypeStruct((256, 128), F32),
    ]
    results = pl.pallas_call(
        kernel,
        out_shape=shapes,
        in_specs=[hbm] * 7 + [vmem, pl.BlockSpec(memory_space=pltpu.SMEM)],
        out_specs=[vmem] * 4,
        scratch_shapes=[
            pltpu.VMEM((256, width), BF16),
            pltpu.VMEM((112, 2688), BF16),
            pltpu.VMEM((56, width), BF16),
            pltpu.VMEM((256, width), BF16),
            pltpu.VMEM((256, 2, 128), F32),
            pltpu.VMEM((256, 2, 128), F32),
            pltpu.VMEM((256, 2, 128), F32),
            pltpu.VMEM((256, 128), F32),
            pltpu.VMEM((16, 128), F32),
            pltpu.VMEM((16, 128), F32),
            pltpu.VMEM((pieces, 16, 128), F32),
            pltpu.VMEM((256, 128), F32),
            pltpu.VMEM((ROWS, 256), BF16),
            pltpu.VMEM((NX * 112, 768), BF16),
            pltpu.VMEM((NX, 592, 128), BF16),
            pltpu.VMEM((NX * NY, 592, 128), BF16),
            pltpu.VMEM((NX * NY, 112, 768), BF16),
            pltpu.VMEM((NX, ROWS, width), BF16),
            pltpu.VMEM((NX, ROWS, width), BF16),
            pltpu.VMEM((NY, 112, 896), BF16),
            pltpu.VMEM((256, width), BF16),
            pltpu.VMEM((NX, ROWS, 768), BF16),
            pltpu.VMEM((NX, ROWS, 256), BF16),
            pltpu.VMEM((NX, ROWS, width), BF16),
            pltpu.VMEM((2, ROWS, width), BF16),
            pltpu.VMEM((2, HALF, width), BF16),
            pltpu.VMEM((NY, 112, 896), BF16),
            pltpu.VMEM((NY, 112, 896), BF16),
            pltpu.VMEM((112, 896), BF16),
            sem((NX,)), sem((NX,)),
            sem((NX, NY)), sem((NX, NY)), sem((NX,)),
            sem((6,)), sem((6,)), sem((6,)), sem((6,)),
            sem((NY,)), sem((NY,)), sem,
            sem((6,)), sem((6,)), sem((NY,)), sem((NY,)), sem, sem, sem((7,)),
            sem((pieces,)), sem((pieces,)), sem((pieces,)), sem((pieces,)), sem, sem,
            pltpu.SemaphoreType.REGULAR, pltpu.SemaphoreType.REGULAR,
        ],
        compiler_params=pltpu.CompilerParams(
            collective_id=0, has_side_effects=True, vmem_limit_bytes=63 * 1024 * 1024
        ),
        cost_estimate=pl.CostEstimate(flops=100_000_000_000, bytes_accessed=5_000_000, transcendentals=0),
    )(
        patch_rows[0], qkv_weight[0], out_weight[0], cotangent[0], tiled(outer_delta[0]),
        tiled(momentum), tiled(global_params), keep_mask, fragment_index,
    )
    out, grad, new_m, new_p = pl.pallas_call(
        hand_out,
        out_shape=shapes,
        in_specs=[hbm] * 4,
        out_specs=[hbm] * 4,
        scratch_shapes=[pltpu.VMEM(a.shape, a.dtype) for a in shapes] + [sem((2, 7))],
        compiler_params=pltpu.CompilerParams(vmem_limit_bytes=63 * 1024 * 1024),
    )(*results)
    return out[None], grad[None], new_m.reshape(-1), new_p.reshape(-1)


def solution(mesh):
    in_specs = (
        P(("replica", "fsdp"), None, None),
        P("replica", "fsdp", None),
        P("replica", "fsdp", None),
        P(("replica", "fsdp"), None, None),
        P(("replica", "fsdp"), None),
        P("replica", None, "fsdp"),
        P(None, "fsdp"),
        P(None, "fsdp"),
        P(),
    )
    out_specs = (
        P(("replica", "fsdp"), None, None),
        P("replica", "fsdp", None),
        P("fsdp"),
        P("fsdp"),
    )
    return jax.shard_map(
        on_device, mesh=mesh, in_specs=in_specs, out_specs=out_specs, check_vma=False
    )
```

```python
import math

import jax
import jax.numpy as jnp
from jax import lax
from jax.experimental import pallas as pl
from jax.experimental.pallas import tpu as pltpu
from jax.sharding import PartitionSpec as P

HSZ = 112
HEADS = 8
KEEP = 154
ROWS = 160
HALF = ROWS // 2
NX = 4
NY = 4
EPS = 1e-06
MESH = pl.DeviceIdType.MESH
F32 = jnp.float32
BF16 = jnp.bfloat16


def dot(a, b, dims=(((1,), (0,)), ((), ()))):
    return lax.dot_general(a, b, dims, preferred_element_type=F32)


def kernel(
    patch_hbm, qkvw_hbm, outw_hbm, cot_hbm, delta_hbm, mom_hbm, par_hbm, mask_ref, index_ref,
    out_ref, grad_ref, newm_ref, newp_ref,
    patch_ref, qkvw_ref, outw_ref, cot_ref, delta_ref, mom_ref, par_ref,
    local, piece, from_y, parts, total,
    pick, wide, wpack, wbuf, whole_w, act, cotb, oraw, owbuf, qkv, att, lo_send, lo_recv, lo_mid, g_send, g_recv, g_mid,
    wx_s, wx_r, wy_s, wy_r, ax_s, ax_r, cx_s, cx_r, oy_s, oy_r,
    lx_s, lx_r, gy_s, gy_r, gm_s, gm_r, in_s, z1_s, z1_r, z2_s, z2_r, yh_s, yh_r, below, above,
):
    r = lax.axis_index("replica")
    f = lax.axis_index("fsdp")
    x, y = f // NY, lax.rem(f, NY)
    pieces = lax.axis_size("replica") // 2
    own = r // 4 * 2 + lax.rem(r, 2)
    y_hi = lax.rem(r // 2, 2)
    z, nz = r // 4, lax.axis_size("replica") // 4

    loads = [
        pltpu.make_async_copy(src, dst, in_s.at[i])
        for i, (src, dst) in enumerate(
            [
                (qkvw_hbm, qkvw_ref), (patch_hbm, patch_ref), (outw_hbm, outw_ref), (cot_hbm, cot_ref),
                (delta_hbm, delta_ref), (mom_hbm, mom_ref), (par_hbm, par_ref),
            ]
        )
    ]
    for i in (0, 4, 1, 3, 2, 5, 6):
        loads[i].start()

    def at_x(k):
        return lax.rem(x + k, NX)

    def at_y(k):
        return lax.rem(y + k, NY)

    def dev_x(k):
        return (r, at_x(k) * NY + y)

    def dev_y(yy):
        return (r, x * NY + yy)

    def dev_p(k):
        to = lax.rem(own + k, pieces)
        return (to // 2 * 4 + y_hi * 2 + lax.rem(to, 2), f)

    def remote(src, dst, s, t, dev):
        return pltpu.make_async_remote_copy(
            src_ref=src, dst_ref=dst, send_sem=s, recv_sem=t, device_id=dev, device_id_type=MESH
        )

    barrier = pltpu.get_barrier_semaphore()
    partners = [dev_x(k) for k in (1, 2, 3)] + [dev_y(at_y(k)) for k in (1, 2, 3)]
    partners += [(r + 2 - 4 * y_hi, f), (r + 1 - 2 * lax.rem(r, 2), f)]
    for dev in partners:
        pl.semaphore_signal(barrier, inc=1, device_id=dev, device_id_type=MESH)

    def tell(sem, dev):
        pl.semaphore_signal(sem, inc=1, device_id=dev, device_id_type=MESH)

    pl.when(z > 0)(lambda: tell(barrier, (r - 4, f)))
    pl.when(z < nz - 1)(lambda: tell(barrier, (r + 4, f)))

    def from_below():
        pl.when(z > 0)(lambda: pl.semaphore_wait(below, 1))
        pl.when(z < nz - 1)(lambda: tell(below, (r + 4, f)))

    def from_above(p):
        def step():
            if p > 0:
                pl.semaphore_wait(above, 1)
            if p < nz - 1:
                tell(above, (r - 4, f))

        pl.when(z == nz - 1 - p)(step)

    def one_hot(shape, of):
        row = lax.broadcasted_iota(jnp.int32, shape, 0)
        return jnp.where(of(row, lax.broadcasted_iota(jnp.int32, shape, 1)), 1.0, 0.0).astype(BF16)

    loads[0].wait()
    for k in range(NX):
        start = min(224 * k // 128, 4) * 128
        shift = 224 * k - start
        chosen = one_hot(
            (384, 256), lambda i, j: (i == shift + 112 * (j // 128) + j % 128) & (j % 128 < 112)
        )
        for t in range(3):
            cols = qkvw_ref[:, 896 * t + start : 896 * t + start + 384]
            wide[112 * k : 112 * k + 112, 256 * t : 256 * t + 256] = dot(cols, chosen).astype(BF16)
    spread6 = one_hot(
        (128, 768),
        lambda i, j: ((j < 640) & (j % 128 >= 112) & (i == 16 * (j // 128) + j % 128 - 112))
        | ((j >= 640) & (i == 80 + j % 32)),
    )
    filled = dot(wide[:, 640:768], spread6)
    fold = one_hot((32, 112), lambda i, j: (i < 28) & (j % 28 == i))
    group = (
        lax.broadcasted_iota(jnp.int32, (112, 128), 0) // 28
        == lax.broadcasted_iota(jnp.int32, (112, 128), 1) // 32
    )
    for k in range(NX):
        rows = slice(112 * k, 112 * k + 112)
        for t in range(5):
            lanes = slice(128 * t, 128 * t + 128)
            wpack[k, 112 * t : 112 * t + 112, :] = (
                wide[rows, lanes].astype(F32) + filled[rows, lanes]
            ).astype(BF16)
        rest = jnp.where(group, filled[rows, 640:768], 0.0).astype(BF16)
        wpack[k, 560:592, :] = dot(fold, rest).astype(BF16)
    wbuf[f] = wpack[x]

    def synced(ref):
        return jnp.where(jnp.full((256, 128), index_ref[0], jnp.int32) == 0, ref[:, 0, :], ref[:, 1, :])


    def rows_of(k):
        return pl.ds(pl.multiple_of(16 * lax.rem(own + k, pieces), 16), 16)

    def part_out(k):
        at = pieces - k
        return remote(local.at[rows_of(k)], parts.at[at], z1_s.at[k], z1_r.at[at], dev_p(k))

    def part_in(k):
        return remote(parts.at[k], parts.at[k], z1_s.at[pieces - k], z1_r.at[k], dev_p(k))

    def sum_out(k):
        mine = total.at[rows_of(0)]
        return remote(mine, mine, z2_s.at[k], z2_r.at[pieces - k], dev_p(k))

    def sum_in(k):
        theirs = total.at[rows_of(k)]
        return remote(theirs, theirs, z2_s.at[pieces - k], z2_r.at[k], dev_p(k))

    over_y = remote(piece, from_y, yh_s, yh_r, (r + 2 - 4 * y_hi, f))
    beside = jnp.where((z > 0) & (z < nz - 1), 2, 1)
    pl.semaphore_wait(barrier, len(partners) + beside)
    from_below()
    from_above(0)

    def w_x(k):
        return remote(wpack.at[at_x(k)], wbuf.at[f], wx_s.at[k], wx_r.at[NX - k], dev_x(k))

    def w_x_in(k):
        slot = wbuf.at[at_x(k) * NY + y]
        return remote(slot, slot, wx_s.at[NX - k], wx_r.at[k], dev_x(k))

    def along_y(buf, send, recv):
        def down(src, i):
            return remote(buf(src), buf(src), send(i), recv(src), dev_y(y - 1))

        def up(src, i):
            return remote(buf(src), buf(src), send(i), recv(src), dev_y(y + 1))

        def can_down(d):
            return (y > 0) & (y + d < NY)

        def can_up(d):
            return (y < NY - 1) & (y >= d)

        def start():
            pl.when(can_down(0))(lambda: down(y, 0).start())
            pl.when(can_up(0))(lambda: up(y, 1).start())

        def forward(d):
            def pass_down():
                down(y + d, 2 * d).wait_recv()
                down(y + d, 2 * d).start()

            def pass_up():
                up(y - d, 2 * d + 1).wait_recv()
                up(y - d, 2 * d + 1).start()

            pl.when(can_down(d))(pass_down)
            pl.when(can_up(d))(pass_up)

        def finish():
            def low_end():
                for src in (1, 2, 3):
                    up(src, 0).wait_recv()

            def high_end():
                for src in (2, 1, 0):
                    down(src, 0).wait_recv()

            pl.when(y == 0)(low_end)
            pl.when(y == NY - 1)(high_end)

        def drain():
            for d in range(3):
                pl.when(can_down(d))(lambda d=d: down(y, 2 * d).wait_send())
                pl.when(can_up(d))(lambda d=d: up(y, 2 * d + 1).wait_send())

        return start, forward, finish, drain

    w_y = [
        along_y(
            lambda yy, k=k: wbuf.at[at_x(k) * NY + yy],
            lambda j, k=k: wy_s.at[k, j],
            lambda yy, k=k: wy_r.at[k, yy],
        )
        for k in range(NX)
    ]
    o_y = along_y(lambda yy: oraw.at[yy], lambda j: oy_s.at[j], lambda yy: oy_r.at[yy])

    for k in (2, 1, 3):
        w_x(k).start()
    w_y[0][0]()
    from_above(1)

    mask = mask_ref[...]
    n = mask.shape[1]
    upper = (
        lax.broadcasted_iota(jnp.int32, (n, n), 0) <= lax.broadcasted_iota(jnp.int32, (n, n), 1)
    )
    place = dot(
        jnp.broadcast_to(mask, (16, n)).astype(F32).astype(BF16),
        jnp.where(upper, 1.0, 0.0).astype(BF16),
    )[0:1, :].astype(jnp.int32)
    place = jnp.where(mask > 0, place - 1, -1)
    pick[...] = jnp.where(
        lax.broadcasted_iota(jnp.int32, (ROWS, n), 0) == place, 1.0, 0.0
    ).astype(BF16)
    loads[1].wait()
    kept = dot(pick[...], patch_ref[...])
    shifted = kept - jnp.mean(kept, axis=-1, keepdims=True)
    spread = jnp.mean(shifted * shifted, axis=-1, keepdims=True)
    act[x] = (shifted * lax.rsqrt(spread + EPS)).astype(BF16)

    low, high = pl.ds(0, HALF), pl.ds(HALF, HALF)

    def along_x(buf, send, recv):
        def move(i, who, rows, to):
            return remote(buf.at[who, rows], buf.at[who, rows], send.at[i], recv.at[i], dev_x(to))

        def own():
            return [move(0, x, low, 1), move(1, x, high, 3), move(2, x, high, 1), move(3, x, low, 3)]

        def passing():
            return [move(4, at_x(3), low, 1), move(5, at_x(1), high, 3)]

        def incoming():
            return [
                move(0, at_x(3), low, 3), move(1, at_x(1), high, 1),
                move(2, at_x(3), high, 3), move(3, at_x(1), low, 1),
                move(4, at_x(2), low, 2), move(5, at_x(2), high, 2),
            ]

        def start():
            for c in own():
                c.start()

        def forward():
            got = incoming()
            for i in (0, 1):
                got[i].wait_recv()
                passing()[i].start()

        def finish():
            for c in incoming()[2:]:
                c.wait_recv()

        def drain():
            for c in own() + passing():
                c.wait_send()

        return start, forward, finish, drain

    a_x = along_x(act, ax_s, ax_r)
    c_x = along_x(cotb, cx_s, cx_r)
    a_x[0]()
    from_above(2)

    for p, k in enumerate((1, 3)):
        w_x_in(k).wait_recv()
        w_y[k][0]()
        from_above(3 + p)
    w_y[0][1](1)
    w_x_in(2).wait_recv()
    w_y[2][0]()
    from_above(5)
    w_y[1][1](1)
    loads[2].wait()
    oraw[y, 0:56, :] = outw_ref[:, 0:896]
    oraw[y, 56:112, :] = outw_ref[:, 896:1792]
    loads[3].wait()
    cotb[x] = dot(pick[...], cot_ref[...]).astype(BF16)
    loads[4].wait()
    local[...] = synced(delta_ref)
    w_y[3][1](1)
    from_above(6)
    w_y[2][1](1)
    a_x[1]()
    c_x[0]()
    for p in range(7, nz):
        from_above(p)
    for k in range(1, pieces):
        part_out(k).start()
    for k in (0, 1, 3):
        w_y[k][1](2)
    w_y[2][1](2)
    o_y[0]()
    mine = local[rows_of(0), :]
    for k in range(1, pieces):
        part_in(k).wait_recv()
        mine = mine + parts[k]
    piece[...] = mine
    over_y.start()
    c_x[1]()

    a_x[2]()
    width = act.shape[2]
    unfold = one_hot((112, 32), lambda i, j: i % 28 == j)
    back = one_hot((128, 128), lambda i, j: (j < 32) & (i % 32 == j))

    for k in (0, 1, 3, 2):
        w_y[k][2]()

        def unpack(j, carry, k=k):
            at = at_x(k) * NY + j
            for t in range(5):
                whole_w[at, :, 128 * t : 128 * t + 128] = wbuf[at, 112 * t : 112 * t + 112, :]
            rest = jnp.where(group, dot(unfold, wbuf[at, 560:592, :]), 0.0).astype(BF16)
            whole_w[at, :, 640:768] = dot(rest, back).astype(BF16)
            return carry

        lax.fori_loop(0, NY, unpack, 0)
    qkv[...] = dot(
        act[...].reshape(NX * ROWS, width), whole_w[...].reshape(width, 768)
    ).astype(BF16).reshape(NX, ROWS, 768)
    o_y[1](1)
    over_y.wait_recv()
    total[rows_of(0), :] = piece[...] + from_y[...]
    for k in range(1, pieces):
        sum_out(k).start()
    sixth = one_hot(
        (768, 128),
        lambda i, j: ((i < 640) & (i % 128 >= 112) & (j == 16 * (i // 128) + i % 128 - 112))
        | ((i >= 640) & (i < 672) & (j == i - 560)),
    )

    def attend(i):
        for h in range(2):
            q = qkv[i, :, 128 * h : 128 * h + 128]
            q = jnp.where(lax.broadcasted_iota(jnp.int32, (ROWS, 128), 1) < HSZ, q, jnp.zeros_like(q))
            key = qkv[i, :, 256 + 128 * h : 384 + 128 * h]
            val = qkv[i, :, 512:640] if h == 0 else dot(qkv[i], sixth).astype(BF16)
            scores = dot(q, key, (((1,), (1,)), ((), ()))) * (1.0 / math.sqrt(HSZ))
            col = lax.broadcasted_iota(jnp.int32, (ROWS, ROWS), 1)
            scores = jnp.where(col < KEEP, scores, -1e30)
            expo = jnp.exp(scores - jnp.max(scores, axis=-1, keepdims=True))
            probs = (expo / jnp.sum(expo, axis=-1, keepdims=True)).astype(BF16)
            att[i, :, 128 * h : 128 * h + 128] = dot(probs, val).astype(BF16)

    for k in (0, 1):
        attend(at_x(k))
    o_y[1](2)
    for k in (2, 3):
        attend(at_x(k))
    c_x[2]()
    terms = dot(
        att[...].reshape(NX * ROWS, 256), cotb[...].reshape(NX * ROWS, width), (((0,), (0,)), ((), ()))
    ).astype(BF16)
    for j in range(NY):
        rows = slice(128 * (j // 2) + 56 * (j % 2), 128 * (j // 2) + 56 * (j % 2) + 56)
        g_send[j, 0:56, :] = terms[rows, 0:896]
        g_send[j, 56:112, :] = terms[rows, 896:1792]

    o_y[2]()
    for j in range(NY):
        rows = slice(128 * (j // 2) + 56 * (j % 2), 128 * (j // 2) + 56 * (j % 2) + 56)
        owbuf[rows, 0:896] = oraw[j, 0:56, :]
        owbuf[rows, 896:1792] = oraw[j, 56:112, :]
    for h in range(2):
        owbuf[128 * h + 112 : 128 * h + 128, :] = jnp.zeros((16, width), BF16)

    def project(k):
        lo_send[at_x(k)] = dot(att[at_x(k)], owbuf[...]).astype(BF16)

    def lo(i, src, dst, to):
        return remote(src, dst, lx_s.at[i], lx_r.at[i], dev_x(to))

    right, left, over = at_x(1), at_x(3), at_x(2)
    lo_far = [
        lo(0, lo_send.at[over, low], lo_mid.at[0], 1), lo(1, lo_send.at[over, high], lo_mid.at[1], 3)
    ]
    lo_own = [
        lo(2, lo_send.at[right, high], lo_recv.at[0, high], 1),
        lo(3, lo_send.at[left, low], lo_recv.at[1, low], 3),
    ]
    lo_both = [
        lo(4, lo_send.at[right, low], lo_recv.at[0, low], 1),
        lo(5, lo_send.at[left, high], lo_recv.at[1, high], 3),
    ]
    project(2)
    for c in lo_far:
        c.start()
    project(1)
    lo_own[0].start()
    project(3)
    lo_own[1].start()

    def g(k):
        return remote(g_send.at[at_y(k)], g_recv.at[NY - k], gy_s.at[k], gy_r.at[NY - k], dev_y(at_y(k)))

    def g_in(k):
        return remote(g_recv.at[k], g_recv.at[k], gy_s.at[NY - k], gy_r.at[k], dev_y(at_y(k)))

    def g_far(to, via):
        return remote(g_send.at[to], g_mid, gm_s, gm_r, dev_y(via))

    ends = (y == 0) | (y == NY - 1)
    pl.when(y == 0)(lambda: g_far(3, 1).start())
    pl.when(y == 3)(lambda: g_far(0, 2).start())

    def near_y(k):
        return jnp.abs(at_y(k) - y) < 2

    for k in (1, 3):
        pl.when(near_y(k))(lambda k=k: g(k).start())
    pl.when(ends)(lambda: g(2).start())

    lo_far[0].wait_recv()
    lo_send[right, low] = (lo_send[right, low].astype(F32) + lo_mid[0].astype(F32)).astype(BF16)
    lo_both[0].start()
    lo_far[1].wait_recv()
    lo_send[left, high] = (lo_send[left, high].astype(F32) + lo_mid[1].astype(F32)).astype(BF16)
    lo_both[1].start()

    def g_pass():
        to = jnp.where(y == 1, 3, 0)
        g_far(0, 2).wait_recv()
        g_send[to] = (g_send[to].astype(F32) + g_mid[...].astype(F32)).astype(BF16)
        g(2).start()

    pl.when(jnp.logical_not(ends))(g_pass)
    project(0)

    for k in range(1, pieces):
        sum_in(k).wait_recv()
    loads[5].wait()
    loads[6].wait()
    average = total[...] / lax.axis_size("replica")
    new_m = 0.9 * synced(mom_ref) + average
    newm_ref[...] = new_m
    newp_ref[...] = synced(par_ref) - 0.7 * (average + 0.9 * new_m)

    whole = g_send[y].astype(F32)
    g_in(2).wait_recv()
    whole = whole + g_recv[2].astype(F32)
    grad_ref[:, 0:896] = whole[0:56, :]
    grad_ref[:, 896:1792] = whole[56:112, :]
    for k in (1, 3):

        def add(k=k):
            g_in(k).wait_recv()
            grad_ref[:, 0:896] += g_recv[k, 0:56].astype(F32)
            grad_ref[:, 896:1792] += g_recv[k, 56:112].astype(F32)

        pl.when(near_y(k))(add)

    for i in (0, 1):
        lo_own[i].wait_recv()
    for i in (0, 1):
        lo_both[i].wait_recv()
    result = lo_send[x].astype(F32) + lo_recv[0].astype(F32) + lo_recv[1].astype(F32)
    out_ref[...] = dot(pick[...], result.astype(BF16), (((0,), (0,)), ((), ()))).astype(BF16)

    for k in (1, 2, 3):
        w_x(k).wait_send()
    for c in lo_far + lo_own + lo_both:
        c.wait_send()
    for k in range(1, pieces):
        part_out(k).wait_send()
        sum_out(k).wait_send()
    over_y.wait_send()
    for k in (1, 3):
        pl.when(near_y(k))(lambda k=k: g(k).wait_send())
    g(2).wait_send()
    pl.when(ends)(lambda: g_far(0, 1).wait_send())
    for k in range(NX):
        w_y[k][3]()
    o_y[3]()
    a_x[3]()
    c_x[3]()


def hand_out(out_in, grad_in, newm_in, newp_in, out_ref, grad_ref, newm_ref, newp_ref, out_v, grad_v, m_v, p_v, sems):
    steps = [(out_in, out_v, out_ref, pl.ds(64 * i, 64)) for i in range(4)]
    steps += [(grad_in, grad_v, grad_ref, pl.ds(0, 56))]
    steps += [(newm_in, m_v, newm_ref, pl.ds(0, 256)), (newp_in, p_v, newp_ref, pl.ds(0, 256))]
    loads, stores = [], []
    for i, (src, held, dst, rows) in enumerate(steps):
        loads.append(pltpu.make_async_copy(src.at[rows], held.at[rows], sems.at[0, i]))
        stores.append(pltpu.make_async_copy(held.at[rows], dst.at[rows], sems.at[1, i]))
    for c in loads:
        c.start()
    for load, store in zip(loads, stores):
        load.wait()
        store.start()
    for c in stores:
        c.wait()


def on_device(
    patch_rows, qkv_weight, out_weight, cotangent, keep_mask, outer_delta, momentum, global_params,
    fragment_index,
):
    def tiled(rows):
        return rows.reshape(2, 256, 128).transpose(1, 0, 2)

    pieces = lax.axis_size("replica") // 2
    width = patch_rows.shape[2]
    vmem = pl.BlockSpec(memory_space=pltpu.VMEM)
    hbm = pl.BlockSpec(memory_space=pltpu.HBM)
    sem = pltpu.SemaphoreType.DMA
    shapes = [
        jax.ShapeDtypeStruct((256, width), BF16),
        jax.ShapeDtypeStruct((56, width), F32),
        jax.ShapeDtypeStruct((256, 128), F32),
        jax.ShapeDtypeStruct((256, 128), F32),
    ]
    results = pl.pallas_call(
        kernel,
        out_shape=shapes,
        in_specs=[hbm] * 7 + [vmem, pl.BlockSpec(memory_space=pltpu.SMEM)],
        out_specs=[vmem] * 4,
        scratch_shapes=[
            pltpu.VMEM((256, width), BF16),
            pltpu.VMEM((112, 2688), BF16),
            pltpu.VMEM((56, width), BF16),
            pltpu.VMEM((256, width), BF16),
            pltpu.VMEM((256, 2, 128), F32),
            pltpu.VMEM((256, 2, 128), F32),
            pltpu.VMEM((256, 2, 128), F32),
            pltpu.VMEM((256, 128), F32),
            pltpu.VMEM((16, 128), F32),
            pltpu.VMEM((16, 128), F32),
            pltpu.VMEM((pieces, 16, 128), F32),
            pltpu.VMEM((256, 128), F32),
            pltpu.VMEM((ROWS, 256), BF16),
            pltpu.VMEM((NX * 112, 768), BF16),
            pltpu.VMEM((NX, 592, 128), BF16),
            pltpu.VMEM((NX * NY, 592, 128), BF16),
            pltpu.VMEM((NX * NY, 112, 768), BF16),
            pltpu.VMEM((NX, ROWS, width), BF16),
            pltpu.VMEM((NX, ROWS, width), BF16),
            pltpu.VMEM((NY, 112, 896), BF16),
            pltpu.VMEM((256, width), BF16),
            pltpu.VMEM((NX, ROWS, 768), BF16),
            pltpu.VMEM((NX, ROWS, 256), BF16),
            pltpu.VMEM((NX, ROWS, width), BF16),
            pltpu.VMEM((2, ROWS, width), BF16),
            pltpu.VMEM((2, HALF, width), BF16),
            pltpu.VMEM((NY, 112, 896), BF16),
            pltpu.VMEM((NY, 112, 896), BF16),
            pltpu.VMEM((112, 896), BF16),
            sem((NX,)), sem((NX,)),
            sem((NX, 6)), sem((NX, NY)),
            sem((6,)), sem((6,)), sem((6,)), sem((6,)),
            sem((6,)), sem((NY,)),
            sem((6,)), sem((6,)), sem((NY,)), sem((NY,)), sem, sem, sem((7,)),
            sem((pieces,)), sem((pieces,)), sem((pieces,)), sem((pieces,)), sem, sem,
            pltpu.SemaphoreType.REGULAR, pltpu.SemaphoreType.REGULAR,
        ],
        compiler_params=pltpu.CompilerParams(
            collective_id=0, has_side_effects=True, vmem_limit_bytes=63 * 1024 * 1024
        ),
        cost_estimate=pl.CostEstimate(flops=100_000_000_000, bytes_accessed=5_000_000, transcendentals=0),
    )(
        patch_rows[0], qkv_weight[0], out_weight[0], cotangent[0], tiled(outer_delta[0]),
        tiled(momentum), tiled(global_params), keep_mask, fragment_index,
    )
    out, grad, new_m, new_p = pl.pallas_call(
        hand_out,
        out_shape=shapes,
        in_specs=[hbm] * 4,
        out_specs=[hbm] * 4,
        scratch_shapes=[pltpu.VMEM(a.shape, a.dtype) for a in shapes] + [sem((2, 7))],
        compiler_params=pltpu.CompilerParams(vmem_limit_bytes=63 * 1024 * 1024),
    )(*results)
    return out[None], grad[None], new_m.reshape(-1), new_p.reshape(-1)


def solution(mesh):
    in_specs = (
        P(("replica", "fsdp"), None, None),
        P("replica", "fsdp", None),
        P("replica", "fsdp", None),
        P(("replica", "fsdp"), None, None),
        P(("replica", "fsdp"), None),
        P("replica", None, "fsdp"),
        P(None, "fsdp"),
        P(None, "fsdp"),
        P(),
    )
    out_specs = (
        P(("replica", "fsdp"), None, None),
        P("replica", "fsdp", None),
        P("fsdp"),
        P("fsdp"),
    )
    return jax.shard_map(
        on_device, mesh=mesh, in_specs=in_specs, out_specs=out_specs, check_vma=False
    )
```

```python
import math

import jax
import jax.numpy as jnp
from jax import lax
from jax.experimental import pallas as pl
from jax.experimental.pallas import tpu as pltpu
from jax.sharding import PartitionSpec as P

HSZ = 112
HEADS = 8
KEEP = 154
ROWS = 160
HALF = ROWS // 2
NX = 4
NY = 4
EPS = 1e-06
MESH = pl.DeviceIdType.MESH
F32 = jnp.float32
BF16 = jnp.bfloat16


def dot(a, b, dims=(((1,), (0,)), ((), ()))):
    return lax.dot_general(a, b, dims, preferred_element_type=F32)


def kernel(
    patch_hbm, qkvw_hbm, outw_hbm, cot_hbm, delta_hbm, mom_hbm, par_hbm, mask_ref, index_ref,
    out_ref, grad_ref, newm_ref, newp_ref,
    patch_ref, qkvw_ref, outw_ref, cot_ref, delta_ref, mom_ref, par_ref,
    local, piece, from_y, parts, total,
    pick, wide, wpack, wbuf, whole_w, act, cotb, oraw, owbuf, qkv, att, lo_send, lo_recv, lo_mid, g_send, g_recv, g_mid,
    wx_s, wx_r, wy_s, wy_r, ax_s, ax_r, cx_s, cx_r, oy_s, oy_r,
    lx_s, lx_r, gy_s, gy_r, gm_s, gm_r, in_s, z1_s, z1_r, z2_s, z2_r, yh_s, yh_r, below, above,
):
    r = lax.axis_index("replica")
    f = lax.axis_index("fsdp")
    x, y = f // NY, lax.rem(f, NY)
    pieces = lax.axis_size("replica") // 2
    own = r // 4 * 2 + lax.rem(r, 2)
    y_hi = lax.rem(r // 2, 2)
    z, nz = r // 4, lax.axis_size("replica") // 4

    loads = [
        pltpu.make_async_copy(src, dst, in_s.at[i])
        for i, (src, dst) in enumerate(
            [
                (qkvw_hbm, qkvw_ref), (patch_hbm, patch_ref), (outw_hbm, outw_ref), (cot_hbm, cot_ref),
                (delta_hbm, delta_ref), (mom_hbm, mom_ref), (par_hbm, par_ref),
            ]
        )
    ]
    for i in (0, 4, 1, 3, 2, 5, 6):
        loads[i].start()

    def at_x(k):
        return lax.rem(x + k, NX)

    def at_y(k):
        return lax.rem(y + k, NY)

    def dev_x(k):
        return (r, at_x(k) * NY + y)

    def dev_y(yy):
        return (r, x * NY + yy)

    def dev_p(k):
        to = lax.rem(own + k, pieces)
        return (to // 2 * 4 + y_hi * 2 + lax.rem(to, 2), f)

    def remote(src, dst, s, t, dev):
        return pltpu.make_async_remote_copy(
            src_ref=src, dst_ref=dst, send_sem=s, recv_sem=t, device_id=dev, device_id_type=MESH
        )

    barrier = pltpu.get_barrier_semaphore()
    partners = [dev_x(k) for k in (1, 2, 3)] + [dev_y(at_y(k)) for k in (1, 2, 3)]
    partners += [(r + 2 - 4 * y_hi, f), (r + 1 - 2 * lax.rem(r, 2), f)]
    for dev in partners:
        pl.semaphore_signal(barrier, inc=1, device_id=dev, device_id_type=MESH)

    def tell(sem, dev):
        pl.semaphore_signal(sem, inc=1, device_id=dev, device_id_type=MESH)

    pl.when(z > 0)(lambda: tell(barrier, (r - 4, f)))
    pl.when(z < nz - 1)(lambda: tell(barrier, (r + 4, f)))

    def from_below():
        pl.when(z > 0)(lambda: pl.semaphore_wait(below, 1))
        pl.when(z < nz - 1)(lambda: tell(below, (r + 4, f)))

    def from_above(p):
        def step():
            if p > 0:
                pl.semaphore_wait(above, 1)
            if p < nz - 1:
                tell(above, (r - 4, f))

        pl.when(z == nz - 1 - p)(step)

    def one_hot(shape, of):
        row = lax.broadcasted_iota(jnp.int32, shape, 0)
        return jnp.where(of(row, lax.broadcasted_iota(jnp.int32, shape, 1)), 1.0, 0.0).astype(BF16)

    loads[0].wait()
    for k in range(NX):
        start = min(224 * k // 128, 4) * 128
        shift = 224 * k - start
        chosen = one_hot(
            (384, 256), lambda i, j: (i == shift + 112 * (j // 128) + j % 128) & (j % 128 < 112)
        )
        for t in range(3):
            cols = qkvw_ref[:, 896 * t + start : 896 * t + start + 384]
            wide[112 * k : 112 * k + 112, 256 * t : 256 * t + 256] = dot(cols, chosen).astype(BF16)
    spread6 = one_hot(
        (128, 768),
        lambda i, j: ((j < 640) & (j % 128 >= 112) & (i == 16 * (j // 128) + j % 128 - 112))
        | ((j >= 640) & (i == 80 + j % 32)),
    )
    filled = dot(wide[:, 640:768], spread6)
    fold = one_hot((32, 112), lambda i, j: (i < 28) & (j % 28 == i))
    group = (
        lax.broadcasted_iota(jnp.int32, (112, 128), 0) // 28
        == lax.broadcasted_iota(jnp.int32, (112, 128), 1) // 32
    )
    for k in range(NX):
        rows = slice(112 * k, 112 * k + 112)
        for t in range(5):
            lanes = slice(128 * t, 128 * t + 128)
            wpack[k, 112 * t : 112 * t + 112, :] = (
                wide[rows, lanes].astype(F32) + filled[rows, lanes]
            ).astype(BF16)
        rest = jnp.where(group, filled[rows, 640:768], 0.0).astype(BF16)
        wpack[k, 560:592, :] = dot(fold, rest).astype(BF16)
    wbuf[f] = wpack[x]

    def synced(ref):
        return jnp.where(jnp.full((256, 128), index_ref[0], jnp.int32) == 0, ref[:, 0, :], ref[:, 1, :])


    def rows_of(k):
        return pl.ds(pl.multiple_of(16 * lax.rem(own + k, pieces), 16), 16)

    def part_out(k):
        at = pieces - k
        return remote(local.at[rows_of(k)], parts.at[at], z1_s.at[k], z1_r.at[at], dev_p(k))

    def part_in(k):
        return remote(parts.at[k], parts.at[k], z1_s.at[pieces - k], z1_r.at[k], dev_p(k))

    def sum_out(k):
        mine = total.at[rows_of(0)]
        return remote(mine, mine, z2_s.at[k], z2_r.at[pieces - k], dev_p(k))

    def sum_in(k):
        theirs = total.at[rows_of(k)]
        return remote(theirs, theirs, z2_s.at[pieces - k], z2_r.at[k], dev_p(k))

    over_y = remote(piece, from_y, yh_s, yh_r, (r + 2 - 4 * y_hi, f))
    beside = jnp.where((z > 0) & (z < nz - 1), 2, 1)
    pl.semaphore_wait(barrier, len(partners) + beside)
    from_below()
    from_above(0)

    def w_x(k):
        return remote(wpack.at[at_x(k)], wbuf.at[f], wx_s.at[k], wx_r.at[NX - k], dev_x(k))

    def w_x_in(k):
        slot = wbuf.at[at_x(k) * NY + y]
        return remote(slot, slot, wx_s.at[NX - k], wx_r.at[k], dev_x(k))

    def along_y(buf, send, recv):
        def down(src, i):
            return remote(buf(src), buf(src), send(i), recv(src), dev_y(y - 1))

        def up(src, i):
            return remote(buf(src), buf(src), send(i), recv(src), dev_y(y + 1))

        def can_down(d):
            return (y > 0) & (y + d < NY)

        def can_up(d):
            return (y < NY - 1) & (y >= d)

        def start():
            pl.when(can_down(0))(lambda: down(y, 0).start())
            pl.when(can_up(0))(lambda: up(y, 1).start())

        def forward(d):
            def pass_down():
                down(y + d, 2 * d).wait_recv()
                down(y + d, 2 * d).start()

            def pass_up():
                up(y - d, 2 * d + 1).wait_recv()
                up(y - d, 2 * d + 1).start()

            pl.when(can_down(d))(pass_down)
            pl.when(can_up(d))(pass_up)

        def finish():
            def low_end():
                for src in (1, 2, 3):
                    up(src, 0).wait_recv()

            def high_end():
                for src in (2, 1, 0):
                    down(src, 0).wait_recv()

            pl.when(y == 0)(low_end)
            pl.when(y == NY - 1)(high_end)

        def drain():
            for d in range(3):
                pl.when(can_down(d))(lambda d=d: down(y, 2 * d).wait_send())
                pl.when(can_up(d))(lambda d=d: up(y, 2 * d + 1).wait_send())

        return start, forward, finish, drain

    w_y = [
        along_y(
            lambda yy, k=k: wbuf.at[at_x(k) * NY + yy],
            lambda j, k=k: wy_s.at[k, j],
            lambda yy, k=k: wy_r.at[k, yy],
        )
        for k in range(NX)
    ]
    o_y = along_y(lambda yy: oraw.at[yy], lambda j: oy_s.at[j], lambda yy: oy_r.at[yy])

    for k in (1, 3):
        w_x(k).start()
    w_y[0][0]()
    w_x(2).start()
    from_above(1)

    mask = mask_ref[...]
    n = mask.shape[1]
    upper = (
        lax.broadcasted_iota(jnp.int32, (n, n), 0) <= lax.broadcasted_iota(jnp.int32, (n, n), 1)
    )
    place = dot(
        jnp.broadcast_to(mask, (16, n)).astype(F32).astype(BF16),
        jnp.where(upper, 1.0, 0.0).astype(BF16),
    )[0:1, :].astype(jnp.int32)
    place = jnp.where(mask > 0, place - 1, -1)
    pick[...] = jnp.where(
        lax.broadcasted_iota(jnp.int32, (ROWS, n), 0) == place, 1.0, 0.0
    ).astype(BF16)
    loads[1].wait()
    kept = dot(pick[...], patch_ref[...])
    shifted = kept - jnp.mean(kept, axis=-1, keepdims=True)
    spread = jnp.mean(shifted * shifted, axis=-1, keepdims=True)
    act[x] = (shifted * lax.rsqrt(spread + EPS)).astype(BF16)

    low, high = pl.ds(0, HALF), pl.ds(HALF, HALF)

    def along_x(buf, send, recv):
        def move(i, who, rows, to):
            return remote(buf.at[who, rows], buf.at[who, rows], send.at[i], recv.at[i], dev_x(to))

        def own():
            return [move(0, x, low, 1), move(1, x, high, 3), move(2, x, high, 1), move(3, x, low, 3)]

        def passing():
            return [move(4, at_x(3), low, 1), move(5, at_x(1), high, 3)]

        def incoming():
            return [
                move(0, at_x(3), low, 3), move(1, at_x(1), high, 1),
                move(2, at_x(3), high, 3), move(3, at_x(1), low, 1),
                move(4, at_x(2), low, 2), move(5, at_x(2), high, 2),
            ]

        def start():
            for c in own():
                c.start()

        def forward():
            got = incoming()
            for i in (0, 1):
                got[i].wait_recv()
                passing()[i].start()

        def finish():
            for c in incoming()[2:]:
                c.wait_recv()

        def drain():
            for c in own() + passing():
                c.wait_send()

        return start, forward, finish, drain

    a_x = along_x(act, ax_s, ax_r)
    c_x = along_x(cotb, cx_s, cx_r)
    a_x[0]()
    from_above(2)

    for p, k in enumerate((1, 3)):
        w_x_in(k).wait_recv()
        w_y[k][0]()
        from_above(3 + p)
    w_y[0][1](1)
    w_x_in(2).wait_recv()
    w_y[2][0]()
    from_above(5)
    w_y[1][1](1)
    loads[2].wait()
    oraw[y, 0:56, :] = outw_ref[:, 0:896]
    oraw[y, 56:112, :] = outw_ref[:, 896:1792]
    loads[3].wait()
    cotb[x] = dot(pick[...], cot_ref[...]).astype(BF16)
    loads[4].wait()
    local[...] = synced(delta_ref)
    w_y[3][1](1)
    from_above(6)
    w_y[2][1](1)
    a_x[1]()
    c_x[0]()
    for p in range(7, nz):
        from_above(p)
    for k in range(1, pieces):
        part_out(k).start()
    for k in (0, 1, 3):
        w_y[k][1](2)
    w_y[2][1](2)
    o_y[0]()
    mine = local[rows_of(0), :]
    for k in range(1, pieces):
        part_in(k).wait_recv()
        mine = mine + parts[k]
    piece[...] = mine
    over_y.start()
    c_x[1]()

    a_x[2]()
    width = act.shape[2]
    unfold = one_hot((112, 32), lambda i, j: i % 28 == j)
    back = one_hot((128, 128), lambda i, j: (j < 32) & (i % 32 == j))

    for k in (0, 1, 3, 2):
        w_y[k][2]()

        def unpack(j, carry, k=k):
            at = at_x(k) * NY + j
            for t in range(5):
                whole_w[at, :, 128 * t : 128 * t + 128] = wbuf[at, 112 * t : 112 * t + 112, :]
            rest = jnp.where(group, dot(unfold, wbuf[at, 560:592, :]), 0.0).astype(BF16)
            whole_w[at, :, 640:768] = dot(rest, back).astype(BF16)
            return carry

        lax.fori_loop(0, NY, unpack, 0)
    qkv[...] = dot(
        act[...].reshape(NX * ROWS, width), whole_w[...].reshape(width, 768)
    ).astype(BF16).reshape(NX, ROWS, 768)
    o_y[1](1)
    over_y.wait_recv()
    total[rows_of(0), :] = piece[...] + from_y[...]
    for k in range(1, pieces):
        sum_out(k).start()
    sixth = one_hot(
        (768, 128),
        lambda i, j: ((i < 640) & (i % 128 >= 112) & (j == 16 * (i // 128) + i % 128 - 112))
        | ((i >= 640) & (i < 672) & (j == i - 560)),
    )

    def attend(i):
        for h in range(2):
            q = qkv[i, :, 128 * h : 128 * h + 128]
            q = jnp.where(lax.broadcasted_iota(jnp.int32, (ROWS, 128), 1) < HSZ, q, jnp.zeros_like(q))
            key = qkv[i, :, 256 + 128 * h : 384 + 128 * h]
            val = qkv[i, :, 512:640] if h == 0 else dot(qkv[i], sixth).astype(BF16)
            scores = dot(q, key, (((1,), (1,)), ((), ()))) * (1.0 / math.sqrt(HSZ))
            col = lax.broadcasted_iota(jnp.int32, (ROWS, ROWS), 1)
            scores = jnp.where(col < KEEP, scores, -1e30)
            expo = jnp.exp(scores - jnp.max(scores, axis=-1, keepdims=True))
            probs = (expo / jnp.sum(expo, axis=-1, keepdims=True)).astype(BF16)
            att[i, :, 128 * h : 128 * h + 128] = dot(probs, val).astype(BF16)

    for k in (0, 1):
        attend(at_x(k))
    o_y[1](2)
    for k in (2, 3):
        attend(at_x(k))
    o_y[2]()
    for j in range(NY):
        rows = slice(128 * (j // 2) + 56 * (j % 2), 128 * (j // 2) + 56 * (j % 2) + 56)
        owbuf[rows, 0:896] = oraw[j, 0:56, :]
        owbuf[rows, 896:1792] = oraw[j, 56:112, :]
    for h in range(2):
        owbuf[128 * h + 112 : 128 * h + 128, :] = jnp.zeros((16, width), BF16)

    def project(k):
        lo_send[at_x(k)] = dot(att[at_x(k)], owbuf[...]).astype(BF16)

    def lo(i, src, dst, to):
        return remote(src, dst, lx_s.at[i], lx_r.at[i], dev_x(to))

    right, left, over = at_x(1), at_x(3), at_x(2)
    lo_far = [
        lo(0, lo_send.at[over, low], lo_mid.at[0], 1), lo(1, lo_send.at[over, high], lo_mid.at[1], 3)
    ]
    lo_own = [
        lo(2, lo_send.at[right, high], lo_recv.at[0, high], 1),
        lo(3, lo_send.at[left, low], lo_recv.at[1, low], 3),
    ]
    lo_both = [
        lo(4, lo_send.at[right, low], lo_recv.at[0, low], 1),
        lo(5, lo_send.at[left, high], lo_recv.at[1, high], 3),
    ]
    project(2)
    for c in lo_far:
        c.start()
    project(1)
    lo_own[0].start()
    project(3)
    lo_own[1].start()

    c_x[2]()
    terms = dot(
        att[...].reshape(NX * ROWS, 256), cotb[...].reshape(NX * ROWS, width), (((0,), (0,)), ((), ()))
    ).astype(BF16)
    for j in range(NY):
        rows = slice(128 * (j // 2) + 56 * (j % 2), 128 * (j // 2) + 56 * (j % 2) + 56)
        g_send[j, 0:56, :] = terms[rows, 0:896]
        g_send[j, 56:112, :] = terms[rows, 896:1792]


    def g(k):
        return remote(g_send.at[at_y(k)], g_recv.at[NY - k], gy_s.at[k], gy_r.at[NY - k], dev_y(at_y(k)))

    def g_in(k):
        return remote(g_recv.at[k], g_recv.at[k], gy_s.at[NY - k], gy_r.at[k], dev_y(at_y(k)))

    def g_far(to, via):
        return remote(g_send.at[to], g_mid, gm_s, gm_r, dev_y(via))

    ends = (y == 0) | (y == NY - 1)
    pl.when(y == 0)(lambda: g_far(3, 1).start())
    pl.when(y == 3)(lambda: g_far(0, 2).start())

    def near_y(k):
        return jnp.abs(at_y(k) - y) < 2

    for k in (1, 3):
        pl.when(near_y(k))(lambda k=k: g(k).start())
    pl.when(ends)(lambda: g(2).start())

    lo_far[0].wait_recv()
    lo_send[right, low] = (lo_send[right, low].astype(F32) + lo_mid[0].astype(F32)).astype(BF16)
    lo_both[0].start()
    lo_far[1].wait_recv()
    lo_send[left, high] = (lo_send[left, high].astype(F32) + lo_mid[1].astype(F32)).astype(BF16)
    lo_both[1].start()

    def g_pass():
        to = jnp.where(y == 1, 3, 0)
        g_far(0, 2).wait_recv()
        g_send[to] = (g_send[to].astype(F32) + g_mid[...].astype(F32)).astype(BF16)
        g(2).start()

    pl.when(jnp.logical_not(ends))(g_pass)
    project(0)

    for k in range(1, pieces):
        sum_in(k).wait_recv()
    loads[5].wait()
    loads[6].wait()
    average = total[...] / lax.axis_size("replica")
    new_m = 0.9 * synced(mom_ref) + average
    newm_ref[...] = new_m
    newp_ref[...] = synced(par_ref) - 0.7 * (average + 0.9 * new_m)

    whole = g_send[y].astype(F32)
    g_in(2).wait_recv()
    whole = whole + g_recv[2].astype(F32)
    grad_ref[:, 0:896] = whole[0:56, :]
    grad_ref[:, 896:1792] = whole[56:112, :]
    for k in (1, 3):

        def add(k=k):
            g_in(k).wait_recv()
            grad_ref[:, 0:896] += g_recv[k, 0:56].astype(F32)
            grad_ref[:, 896:1792] += g_recv[k, 56:112].astype(F32)

        pl.when(near_y(k))(add)

    for i in (0, 1):
        lo_own[i].wait_recv()
    for i in (0, 1):
        lo_both[i].wait_recv()
    result = lo_send[x].astype(F32) + lo_recv[0].astype(F32) + lo_recv[1].astype(F32)
    out_ref[...] = dot(pick[...], result.astype(BF16), (((0,), (0,)), ((), ()))).astype(BF16)

    for k in (1, 2, 3):
        w_x(k).wait_send()
    for c in lo_far + lo_own + lo_both:
        c.wait_send()
    for k in range(1, pieces):
        part_out(k).wait_send()
        sum_out(k).wait_send()
    over_y.wait_send()
    for k in (1, 3):
        pl.when(near_y(k))(lambda k=k: g(k).wait_send())
    g(2).wait_send()
    pl.when(ends)(lambda: g_far(0, 1).wait_send())
    for k in range(NX):
        w_y[k][3]()
    o_y[3]()
    a_x[3]()
    c_x[3]()


def hand_out(out_in, grad_in, newm_in, newp_in, out_ref, grad_ref, newm_ref, newp_ref, out_v, grad_v, m_v, p_v, sems):
    steps = [(out_in, out_v, out_ref, pl.ds(64 * i, 64)) for i in range(4)]
    steps += [(grad_in, grad_v, grad_ref, pl.ds(0, 56))]
    steps += [(newm_in, m_v, newm_ref, pl.ds(0, 256)), (newp_in, p_v, newp_ref, pl.ds(0, 256))]
    loads, stores = [], []
    for i, (src, held, dst, rows) in enumerate(steps):
        loads.append(pltpu.make_async_copy(src.at[rows], held.at[rows], sems.at[0, i]))
        stores.append(pltpu.make_async_copy(held.at[rows], dst.at[rows], sems.at[1, i]))
    for c in loads:
        c.start()
    for load, store in zip(loads, stores):
        load.wait()
        store.start()
    for c in stores:
        c.wait()


def on_device(
    patch_rows, qkv_weight, out_weight, cotangent, keep_mask, outer_delta, momentum, global_params,
    fragment_index,
):
    def tiled(rows):
        return rows.reshape(2, 256, 128).transpose(1, 0, 2)

    pieces = lax.axis_size("replica") // 2
    width = patch_rows.shape[2]
    vmem = pl.BlockSpec(memory_space=pltpu.VMEM)
    hbm = pl.BlockSpec(memory_space=pltpu.HBM)
    sem = pltpu.SemaphoreType.DMA
    shapes = [
        jax.ShapeDtypeStruct((256, width), BF16),
        jax.ShapeDtypeStruct((56, width), F32),
        jax.ShapeDtypeStruct((256, 128), F32),
        jax.ShapeDtypeStruct((256, 128), F32),
    ]
    results = pl.pallas_call(
        kernel,
        out_shape=shapes,
        in_specs=[hbm] * 7 + [vmem, pl.BlockSpec(memory_space=pltpu.SMEM)],
        out_specs=[vmem] * 4,
        scratch_shapes=[
            pltpu.VMEM((256, width), BF16),
            pltpu.VMEM((112, 2688), BF16),
            pltpu.VMEM((56, width), BF16),
            pltpu.VMEM((256, width), BF16),
            pltpu.VMEM((256, 2, 128), F32),
            pltpu.VMEM((256, 2, 128), F32),
            pltpu.VMEM((256, 2, 128), F32),
            pltpu.VMEM((256, 128), F32),
            pltpu.VMEM((16, 128), F32),
            pltpu.VMEM((16, 128), F32),
            pltpu.VMEM((pieces, 16, 128), F32),
            pltpu.VMEM((256, 128), F32),
            pltpu.VMEM((ROWS, 256), BF16),
            pltpu.VMEM((NX * 112, 768), BF16),
            pltpu.VMEM((NX, 592, 128), BF16),
            pltpu.VMEM((NX * NY, 592, 128), BF16),
            pltpu.VMEM((NX * NY, 112, 768), BF16),
            pltpu.VMEM((NX, ROWS, width), BF16),
            pltpu.VMEM((NX, ROWS, width), BF16),
            pltpu.VMEM((NY, 112, 896), BF16),
            pltpu.VMEM((256, width), BF16),
            pltpu.VMEM((NX, ROWS, 768), BF16),
            pltpu.VMEM((NX, ROWS, 256), BF16),
            pltpu.VMEM((NX, ROWS, width), BF16),
            pltpu.VMEM((2, ROWS, width), BF16),
            pltpu.VMEM((2, HALF, width), BF16),
            pltpu.VMEM((NY, 112, 896), BF16),
            pltpu.VMEM((NY, 112, 896), BF16),
            pltpu.VMEM((112, 896), BF16),
            sem((NX,)), sem((NX,)),
            sem((NX, 6)), sem((NX, NY)),
            sem((6,)), sem((6,)), sem((6,)), sem((6,)),
            sem((6,)), sem((NY,)),
            sem((6,)), sem((6,)), sem((NY,)), sem((NY,)), sem, sem, sem((7,)),
            sem((pieces,)), sem((pieces,)), sem((pieces,)), sem((pieces,)), sem, sem,
            pltpu.SemaphoreType.REGULAR, pltpu.SemaphoreType.REGULAR,
        ],
        compiler_params=pltpu.CompilerParams(
            collective_id=0, has_side_effects=True, vmem_limit_bytes=63 * 1024 * 1024
        ),
        cost_estimate=pl.CostEstimate(flops=100_000_000_000, bytes_accessed=5_000_000, transcendentals=0),
    )(
        patch_rows[0], qkv_weight[0], out_weight[0], cotangent[0], tiled(outer_delta[0]),
        tiled(momentum), tiled(global_params), keep_mask, fragment_index,
    )
    out, grad, new_m, new_p = pl.pallas_call(
        hand_out,
        out_shape=shapes,
        in_specs=[hbm] * 4,
        out_specs=[hbm] * 4,
        scratch_shapes=[pltpu.VMEM(a.shape, a.dtype) for a in shapes] + [sem((2, 7))],
        compiler_params=pltpu.CompilerParams(vmem_limit_bytes=63 * 1024 * 1024),
    )(*results)
    return out[None], grad[None], new_m.reshape(-1), new_p.reshape(-1)


def solution(mesh):
    in_specs = (
        P(("replica", "fsdp"), None, None),
        P("replica", "fsdp", None),
        P("replica", "fsdp", None),
        P(("replica", "fsdp"), None, None),
        P(("replica", "fsdp"), None),
        P("replica", None, "fsdp"),
        P(None, "fsdp"),
        P(None, "fsdp"),
        P(),
    )
    out_specs = (
        P(("replica", "fsdp"), None, None),
        P("replica", "fsdp", None),
        P("fsdp"),
        P("fsdp"),
    )
    return jax.shard_map(
        on_device, mesh=mesh, in_specs=in_specs, out_specs=out_specs, check_vma=False
    )
```
